128 devices in a mesh: dp: 8 (over x, y_hi), feat: 16 (over y_lo, z, core).
Axes of the slice: x: 4, y: 4 (y_hi: 2, y_lo: 2; y = y_hi * 2 + y_lo), z: 4, core: 2. Of those that a mesh axis runs over, the one named last changes fastest.
Arguments:
- tokens: bfloat16 [8192, 128, 128], P('dp', 'feat'), may hold values from -6 to 6
- cotangent: bfloat16 [8192, 128, 128], P('dp', 'feat'), may hold values from -6 to 6
- left_up_factor: bfloat16 [128, 128, 128], P('feat', 'dp'), may hold values from -0.5 to 0.5
- right_up_factor: bfloat16 [128, 128, 512], P('feat', 'dp'), may hold values from -0.5 to 0.5
- left_out: bfloat16 [128, 512, 128], P('feat', 'dp'), may hold values from -0.25 to 0.25
- right_out: bfloat16 [128, 128, 128], P('feat', 'dp'), may hold values from -0.5 to 0.5
Outputs:
- output: bfloat16 [8192, 128, 128], P('dp', 'feat')
- token_input_gradient: bfloat16 [8192, 128, 128], P('dp', 'feat')
- grad_left_in: float32 [128, 128, 128], P('feat', 'dp')
- grad_right_in: float32 [128, 128, 512], P('feat', 'dp')
- grad_left_out: float32 [128, 512, 128], P('feat', 'dp')
- grad_right_out: float32 [128, 128, 128], P('feat', 'dp')
The draws below stay inside these ranges and needn't reach their ends.
All inputs are finite; a program needn't handle non-finite values.
Results may differ from the reference program's by a relative error of at most 0.0068.
Values may be sent and summed in bfloat16 or wider, within the bound.
A program may use at most 128 MiB of HBM per device.

```python
import jax
import jax.numpy as jnp
from jax import lax

NB = 128
EXPAND = 512
TOKENS = 8192


def shard_levels(key, shape, cuts, smallest, top_value):
    def one(dim, blocks):
        heights = jax.random.uniform(jax.random.fold_in(jax.random.fold_in(key, 6), dim), (blocks,), jnp.float32, smallest / len(cuts), top_value / len(cuts))
        return jnp.repeat(jnp.exp(heights), shape[dim] // blocks).reshape((-1,) + (1,) * (len(shape) - dim - 1))

    factor_of = one(*cuts[0])
    for cut in cuts[1:]:
        factor_of = factor_of * one(*cut)
    return factor_of


def scatter_about(key, dims, spread, limit, cuts=(), held_as=jnp.bfloat16):
    drawn = spread * jax.random.normal(key, dims, jnp.float32)
    if cuts:
        drawn = drawn * shard_levels(key, dims, cuts, -0.22, 0.18)
    return jnp.clip(drawn, -limit, limit).astype(held_as)


def setup_inputs(seed: int = 0) -> dict:
    key_list = jax.random.split(jax.random.key(seed), 7)
    tokens = scatter_about(key_list[0], (TOKENS, NB, NB), 1.0, 6.0, ((0, 8), (1, 16)))
    cotangent = scatter_about(key_list[1], (TOKENS, NB, NB), 1.0, 6.0, ((0, 8), (1, 16)))
    left_up_factor = scatter_about(key_list[2], (NB, NB, NB), NB ** -0.5, 0.5, ((0, 16), (1, 8)))
    right_up_factor = scatter_about(key_list[3], (NB, NB, EXPAND), NB ** -0.5, 0.5, ((0, 16), (1, 8)))
    left_out = scatter_about(key_list[4], (NB, EXPAND, NB), EXPAND ** -0.5, 0.25, ((0, 16), (1, 8)))
    right_out = scatter_about(key_list[5], (NB, NB, NB), NB ** -0.5, 0.5, ((0, 16), (1, 8)))
    return {"tokens": tokens, "cotangent": cotangent, "left_up_factor": left_up_factor, "right_up_factor": right_up_factor, "left_out": left_out, "right_out": right_out}


HIGH = lax.Precision.HIGHEST

def phi_cdf(value):
    return 0.5 * (1.0 + jax.scipy.special.erf(value * 0.7071067811865476))

def gelu_slope(value):
    return phi_cdf(value) + value * jnp.exp(-0.5 * value * value) * 0.3989422804014327

def factor_product(form, first, second):
    return jnp.einsum(form, first.astype(jnp.float32), second.astype(jnp.float32), precision=HIGH)

def block_pass(carry, pieces, left_up_factor, right_up_factor, left_out, right_out):
    source_tokens, upstream = pieces
    mixed_hidden = factor_product('oqj,qjy->oqy', source_tokens, left_up_factor).astype(jnp.bfloat16)
    preactivation = factor_product('vub,buo->vbo', mixed_hidden, right_up_factor)
    active = (preactivation * phi_cdf(preactivation)).astype(jnp.bfloat16)
    folded = factor_product('tce,cef->tcf', active, left_out).astype(jnp.bfloat16)
    result = factor_product('tcf,fcj->tfj', folded, right_out).astype(jnp.bfloat16)
    acc_r2 = factor_product('tcf,tfj->fcj', folded, upstream)
    back_folded = factor_product('tfj,fcj->tcf', upstream, right_out).astype(jnp.bfloat16)
    acc_l2 = factor_product('tce,tcf->cef', active, back_folded)
    preactivation_gradient = (factor_product('tcf,cef->tce', back_folded, left_out) * gelu_slope(preactivation)).astype(jnp.bfloat16)
    right_up_accumulator = factor_product('owk,okq->kwq', mixed_hidden, preactivation_gradient)
    mixed_gradient = factor_product('qyp,ydp->qdy', preactivation_gradient, right_up_factor).astype(jnp.bfloat16)
    left_up_accumulator = factor_product('hlz,hlr->lzr', source_tokens, mixed_gradient)
    source_gradient = factor_product('yfv,fsv->yfs', mixed_gradient, left_up_factor).astype(jnp.bfloat16)
    sums = (carry[0] + left_up_accumulator, carry[1] + right_up_accumulator, carry[2] + acc_l2, carry[3] + acc_r2)
    return (sums, (result, source_gradient))

def reference(tokens, cotangent, left_up_factor, right_up_factor, left_out, right_out):
    rows = TOKENS
    block = 512 if rows % 512 == 0 else rows
    count = rows // block
    shaped = tokens.reshape(count, block, NB, NB)
    upper = cotangent.reshape(count, block, NB, NB)
    start = (jnp.zeros(left_up_factor.shape, jnp.float32), jnp.zeros(right_up_factor.shape, jnp.float32), jnp.zeros(left_out.shape, jnp.float32), jnp.zeros(right_out.shape, jnp.float32))

    def stepper(carry, pieces):
        return block_pass(carry, pieces, left_up_factor, right_up_factor, left_out, right_out)
    sums, (results, backs) = lax.scan(stepper, start, (shaped, upper))
    init_scale = jnp.float32(1.0) / jnp.sqrt(jnp.float32(rows))
    return (results.reshape(rows, NB, NB), backs.reshape(rows, NB, NB), sums[0] * init_scale, sums[1] * init_scale, sums[2] * init_scale, sums[3] * init_scale)
```

```python
import functools

import jax
import jax.numpy as jnp
from jax import lax
from jax.experimental import pallas as pl
from jax.experimental.pallas import tpu as pltpu
from jax.sharding import PartitionSpec as P

MESH = pl.DeviceIdType.MESH
BF = jnp.bfloat16
F32 = jnp.float32
NB = 128
EX = 512
T = 1024
TT = 256
NF = 16
NX = 4
QS = 4
NT = (((1,), (1,)), ((), ()))


def dot(a, b):
    return jnp.dot(a, b, preferred_element_type=F32)


def dot_nt(a, b):
    return lax.dot_general(a, b, NT, preferred_element_type=F32)


def gelu_parts(v):
    bell = jnp.exp2(v * v * (-0.7213475204444817)) * 0.3989422804014327
    t = 1.0 / (1.0 + 0.2316419 * jnp.abs(v))
    poly = 1.330274429 * t - 1.821255978
    poly = poly * t + 1.781477937
    poly = poly * t - 0.356563782
    poly = poly * t + 0.319381530
    tail = bell * (poly * t)
    phi = jnp.where(v >= 0, 1.0 - tail, tail)
    return v * phi, phi + v * bell


def layer(tok_h, cot_h, l_h, r_h, lo_h, r2_h,
          out_h, tg_h, gl_o, gr_o, glo_o, gr2_o,
          tok, cot, lg, rg, log_, r2g,
          a1, a3, a2, a4, s1, s3, s2, s4, z1, z3,
          xc, fc, rt, lot, act, bp, zf, zb, stage_o, stage_t,
          gr_s, glo_s, gl_s, gr2_s, gr_r, glo_r, gl_r, gr2_r,
          gr_y, glo_y, gl_y, gr2_y, gr_yr, glo_yr, gl_yr, gr2_yr,
          in_sem, own_sem, out_sem,
          agy_s, agy_r, agx_s, agx_r, aa_s, aa_r, rx_s, rx_r, ry_s, ry_r):
    dp = lax.axis_index("dp")
    me = lax.axis_index("feat")
    x, yh = lax.div(dp, 2), lax.rem(dp, 2)
    partner = (x * 2 + (1 - yh), me)

    def xpeer(i):
        return (lax.rem(x + i, NX) * 2 + yh, me)

    def fpeer(i):
        return lax.rem(me + i, NF)

    ins = [pltpu.make_async_copy(tok_h, tok, in_sem.at[0]), pltpu.make_async_copy(cot_h, cot, in_sem.at[1])]
    for c in ins:
        c.start()
    facs = [(l_h, lg, 16), (r2_h, r2g, 16), (r_h, rg, 16), (lo_h, log_, 64)]
    own = [pltpu.make_async_copy(sh, g.at[:, pl.ds(pl.multiple_of(dp * n, n), n), :], own_sem.at[k])
           for k, (sh, g, n) in enumerate(facs)]
    for c in own:
        c.start()

    barrier = pltpu.get_barrier_semaphore()

    def greet(i, _):
        pl.semaphore_signal(barrier, inc=1, device_id=(dp, fpeer(i)), device_id_type=MESH)
        return 0

    lax.fori_loop(1, NF, greet, 0)
    for i in range(1, NX):
        pl.semaphore_signal(barrier, inc=1, device_id=xpeer(i), device_id_type=MESH)
    pl.semaphore_signal(barrier, inc=1, device_id=partner, device_id_type=MESH)
    pl.semaphore_wait(barrier, NF - 1 + NX - 1 + 1)

    def remote(src, dst, ss, rs, dev):
        return pltpu.make_async_remote_copy(src_ref=src, dst_ref=dst, send_sem=ss, recv_sem=rs,
                                            device_id=dev, device_id_type=MESH)

    def await_bytes(ref, sem):
        pltpu.make_async_copy(ref, ref, sem).wait()

    for k, (sh, g, n) in enumerate(facs):
        mine = g.at[:, pl.ds(pl.multiple_of(dp * n, n), n), :]
        remote(sh, mine, agy_s.at[k], agy_r.at[k], partner).start()
        for i in range(1, NX):
            remote(sh, mine, agx_s.at[k], agx_r.at[k], xpeer(i)).start()

    def forward_shard(k):
        sh, g, n = facs[k]
        theirs = g.at[:, pl.ds(pl.multiple_of(partner[0] * n, n), n), :]
        await_bytes(theirs, agy_r.at[k])
        for i in range(1, NX):
            remote(theirs, theirs, agx_s.at[k], agx_r.at[k], xpeer(i)).start()

    def gathered(k):
        sh, g, n = facs[k]
        own[k].wait()
        await_bytes(g.at[:, pl.ds(0, 6 * n), :], agx_r.at[k])

    forward_shard(0)
    forward_shard(1)

    def spread(z, a, res, t0):
        for h in range(TT // 128):
            z[t0 // 128 + h, pl.ds(a, NB, stride=8), :] = res[:, h * 128:(h + 1) * 128]

    def send_pair(z, abuf, sbuf, kind, q):
        def one(i, _):
            p = fpeer(i)
            rows = pl.ds(pl.multiple_of(p * 16, 16), 16)
            for tt in range(T // 128):
                piece = z[tt, pl.ds(pl.multiple_of(p * 64 + q * 16, 16), 16), :].astype(BF)
                abuf[q, rows, tt * 128:(tt + 1) * 128] = piece
            return 0

        lax.fori_loop(0, NF, one, 0)
        ship(abuf, sbuf, kind, q)

    def ship(abuf, sbuf, kind, q):
        mine = pl.ds(pl.multiple_of(me * 16, 16), 16)

        def go(i, _):
            p = fpeer(i)
            rows = pl.ds(pl.multiple_of(p * 16, 16), 16)
            remote(abuf.at[q, rows, :], sbuf.at[q, mine, :], aa_s.at[kind, q], aa_r.at[kind, q], (dp, p)).start()
            return 0

        lax.fori_loop(1, NF, go, 0)
        sbuf[q, mine, :] = abuf[q, mine, :]

    def arrived(sbuf, kind, q):
        await_bytes(sbuf.at[q, pl.ds(0, 240), :], aa_r.at[kind, q])

    ins[0].wait()
    gathered(0)
    for a in range(8):
        lt = lg[a].astype(F32).T.astype(BF)
        for t0 in range(0, T, TT):
            spread(z1, a, dot_nt(lt, tok[a, t0:t0 + TT, :]), t0)
    send_pair(z1, a1, s1, 0, 0)
    ins[1].wait()
    gathered(1)
    for f in range(8):
        for t0 in range(0, T, TT):
            spread(z3, f, dot_nt(r2g[f], cot[f, t0:t0 + TT, :]), t0)
    send_pair(z3, a3, s3, 1, 0)
    forward_shard(2)
    forward_shard(3)

    def rest(q, _):
        send_pair(z1, a1, s1, 0, q)
        send_pair(z3, a3, s3, 1, q)
        return 0

    lax.fori_loop(1, QS, rest, 0)
    gathered(2)
    gathered(3)

    def sum_x(k, src, dst, n, lead, sem):
        for i in range(1, NX):
            to = lax.rem(x + i, NX)
            remote(src.at[lead, pl.ds(pl.multiple_of(to * 2 * n, 2 * n), 2 * n), :], dst.at[i - 1, lead],
                   rx_s.at[sem], rx_r.at[sem], xpeer(i)).start()

    scale = 1.0 / jnp.sqrt(F32(8192.0))

    def sum_y(src, dst, ybuf, yrecv, res, n, lead, sem):
        for i in range(NX - 1):
            pass
        await_bytes(dst.at[:, lead], rx_r.at[sem])
        for half in range(2):
            total = src[lead, pl.ds(pl.multiple_of(x * 2 * n + half * n, n), n), :].astype(F32)
            for i in range(NX - 1):
                total += dst[i, lead, half * n:(half + 1) * n, :].astype(F32)

            @pl.when(yh == half)
            def _():
                res[lead] = total

            @pl.when(yh != half)
            def _():
                ybuf[lead] = total.astype(BF)

        remote(ybuf.at[lead], yrecv.at[lead], ry_s.at[sem], ry_r.at[sem], partner).start()

    def finish(yrecv, res, lead, sem):
        await_bytes(yrecv.at[lead], ry_r.at[sem])
        res[lead] = (res[lead] + yrecv[lead].astype(F32)) * scale

    def pair(q, _):
        arrived(s1, 0, q)
        arrived(s3, 1, q)
        for t0 in range(0, T, TT):
            for src, dst in ((s1, xc), (s3, fc)):
                slab = src[q, :, t0:t0 + TT].astype(F32).reshape(NF, 2, 8, TT)
                for h in range(2):
                    dst[h, :, t0:t0 + TT] = slab[:, h].reshape(NB, TT).astype(BF)

        def block(h, _):
            c = q * 2 + h
            rt[...] = rg[c].astype(F32).T.astype(BF)
            lot[...] = log_[c].astype(F32).T.astype(BF)

            def tile(j, _):
                cols = pl.ds(pl.multiple_of(j * TT, TT), TT)
                active, slope = gelu_parts(dot(rt[...], xc[h, :, cols]))
                active = active.astype(BF)
                act[:, cols] = active
                back = (dot(log_[c], fc[h, :, cols]) * slope).astype(BF)
                bp[:, cols] = back
                zf[h, :, cols] = dot(lot[...], active)
                zb[h, :, cols] = dot(rg[c], back)
                return 0

            lax.fori_loop(0, T // TT, tile, 0)
            glo_s[c] = dot_nt(act[...], fc[h]).astype(BF)
            gr_s[c] = dot_nt(xc[h], bp[...]).astype(BF)
            return 0

        lax.fori_loop(0, 2, block, 0)

        for z, abuf, sbuf, kind in ((zf, a2, s2, 2), (zb, a4, s4, 3)):
            def pack(p, _):
                rows = pl.ds(pl.multiple_of(p * 8, 8), 8)
                both = jnp.concatenate([z[0, rows, :], z[1, rows, :]], axis=0)
                abuf[q, pl.ds(pl.multiple_of(p * 16, 16), 16), :] = both.astype(BF)
                return 0

            lax.fori_loop(0, NF, pack, 0)
            ship(abuf, sbuf, kind, q)

        lead = pl.ds(q * 2, 2)
        sum_x(0, gr_s, gr_r, 16, lead, q)
        sum_x(1, glo_s, glo_r, 64, lead, QS + q)

        @pl.when(q > 0)
        def _():
            before = pl.ds(q * 2 - 2, 2)
            sum_y(gr_s, gr_r, gr_y, gr_yr, gr_o, 16, before, q - 1)
            sum_y(glo_s, glo_r, glo_y, glo_yr, glo_o, 64, before, QS + q - 1)

        return 0

    lax.fori_loop(0, QS, pair, 0)

    def gather_rows(sbuf, kind, z):
        def one_q(q, _):
            arrived(sbuf, kind, q)

            def one_k(k, _):
                rows = pl.ds(pl.multiple_of(k * 16, 16), 16)
                for tt in range(T // 128):
                    slab = sbuf[q, rows, tt * 128:(tt + 1) * 128].astype(F32)
                    for h in range(2):
                        z[tt, pl.ds(k * 8 + q * 2 + h, 8, stride=NB), :] = slab[h * 8:(h + 1) * 8]
                return 0

            lax.fori_loop(0, NF, one_k, 0)
            return 0

        lax.fori_loop(0, QS, one_q, 0)

    eye = (lax.broadcasted_iota(jnp.int32, (TT, TT), 0) == lax.broadcasted_iota(jnp.int32, (TT, TT), 1)).astype(BF)

    def block_rows(z, f):
        rows = pl.ds(pl.multiple_of(f * NB, NB), NB)
        return [z[tt, rows, :].astype(BF) for tt in range(T // 128)]

    gather_rows(s2, 2, z1)

    def last_pair():
        lead = pl.ds(QS * 2 - 2, 2)
        sum_y(gr_s, gr_r, gr_y, gr_yr, gr_o, 16, lead, QS - 1)
        sum_y(glo_s, glo_r, glo_y, glo_yr, glo_o, 64, lead, 2 * QS - 1)

    def f_block(f, _):
        y = jnp.concatenate(block_rows(z1, f), axis=1)
        gr2_s[f] = dot(y, cot[f]).astype(BF)
        for t0 in range(0, T, TT):
            yt = dot_nt(eye, y[:, t0:t0 + TT]).astype(BF)
            stage_o[f, t0:t0 + TT, :] = dot(yt, r2g[f]).astype(BF)
        pltpu.make_async_copy(stage_o.at[f], out_h.at[f], out_sem.at[0]).start()
        return 0

    lax.fori_loop(0, 8, f_block, 0)
    every = pl.ds(0, 8)
    sum_x(3, gr2_s, gr2_r, 16, every, 2 * QS)
    last_pair()

    gather_rows(s4, 3, z3)

    def a_grad(a, _):
        m = jnp.concatenate(block_rows(z3, a), axis=1)
        gl_s[a] = dot(m, tok[a]).T.astype(BF)
        return 0

    lax.fori_loop(0, 8, a_grad, 0)
    sum_x(2, gl_s, gl_r, 16, every, 2 * QS + 1)
    sum_y(gr2_s, gr2_r, gr2_y, gr2_yr, gr2_o, 16, every, 2 * QS)

    def a_block(a, _):
        m = jnp.concatenate(block_rows(z3, a), axis=1)
        for t0 in range(0, T, TT):
            mt = dot_nt(eye, m[:, t0:t0 + TT]).astype(BF)
            stage_t[a, t0:t0 + TT, :] = dot_nt(mt, lg[a]).astype(BF)
        pltpu.make_async_copy(stage_t.at[a], tg_h.at[a], out_sem.at[1]).start()
        return 0

    lax.fori_loop(0, 8, a_block, 0)
    sum_y(gl_s, gl_r, gl_y, gl_yr, gl_o, 16, every, 2 * QS + 1)

    def fin(q, _):
        lead = pl.ds(q * 2, 2)
        finish(gr_yr, gr_o, lead, q)
        finish(glo_yr, glo_o, lead, QS + q)
        return 0

    lax.fori_loop(0, QS, fin, 0)
    finish(gr2_yr, gr2_o, every, 2 * QS)
    finish(gl_yr, gl_o, every, 2 * QS + 1)

    for k, (sh, g, n) in enumerate(facs):
        await_bytes(g.at[:, pl.ds(0, n), :], agy_s.at[k])
        await_bytes(g.at[:, pl.ds(0, 6 * n), :], agx_s.at[k])

    def drain(q, _):
        for kind, buf in enumerate((a1, a3, a2, a4)):
            await_bytes(buf.at[q, pl.ds(0, 240), :], aa_s.at[kind, q])
        lead = pl.ds(q * 2, 2)
        await_bytes(gr_r.at[:, lead], rx_s.at[q])
        await_bytes(glo_r.at[:, lead], rx_s.at[QS + q])
        await_bytes(gr_yr.at[lead], ry_s.at[q])
        await_bytes(glo_yr.at[lead], ry_s.at[QS + q])
        return 0

    lax.fori_loop(0, QS, drain, 0)
    await_bytes(gr2_r, rx_s.at[2 * QS])
    await_bytes(gl_r, rx_s.at[2 * QS + 1])
    await_bytes(gr2_yr, ry_s.at[2 * QS])
    await_bytes(gl_yr, ry_s.at[2 * QS + 1])
    await_bytes(stage_o, out_sem.at[0])
    await_bytes(stage_t, out_sem.at[1])


def on_device(tokens, cotangent, left_up, right_up, left_out, right_out):
    any_, vm = pl.BlockSpec(memory_space=pl.ANY), pl.BlockSpec(memory_space=pltpu.VMEM)
    V, D = pltpu.VMEM, pltpu.SemaphoreType.DMA
    slab = V((QS, NF * 16, T), BF)
    scratch = [
        V((8, T, NB), BF), V((8, T, NB), BF),
        V((8, NB, NB), BF), V((8, NB, EX), BF), V((8, EX, NB), BF), V((8, NB, NB), BF),
        slab, slab, slab, slab, slab, slab, slab, slab,
        V((T // 128, 1024, 128), F32), V((T // 128, 1024, 128), F32),
        V((2, NB, T), BF), V((2, NB, T), BF), V((EX, NB), BF), V((NB, EX), BF),
        V((EX, T), BF), V((EX, T), BF), V((2, NB, T), F32), V((2, NB, T), F32),
        V((8, T, NB), BF), V((8, T, NB), BF),
        V((8, NB, EX), BF), V((8, EX, NB), BF), V((8, NB, NB), BF), V((8, NB, NB), BF),
        V((3, 8, 32, EX), BF), V((3, 8, 128, NB), BF), V((3, 8, 32, NB), BF), V((3, 8, 32, NB), BF),
        V((8, 16, EX), BF), V((8, 64, NB), BF), V((8, 16, NB), BF), V((8, 16, NB), BF),
        V((8, 16, EX), BF), V((8, 64, NB), BF), V((8, 16, NB), BF), V((8, 16, NB), BF),
        D((2,)), D((4,)), D((2,)),
        D((4,)), D((4,)), D((4,)), D((4,)), D((4, QS)), D((4, QS)),
        D((2 * QS + 2,)), D((2 * QS + 2,)), D((2 * QS + 2,)), D((2 * QS + 2,)),
    ]
    S = jax.ShapeDtypeStruct
    out, tg, gl, gr, glo, gr2 = pl.pallas_call(
        layer,
        out_shape=(S((8, T, NB), BF), S((8, T, NB), BF), S((8, 16, NB), F32), S((8, 16, EX), F32),
                   S((8, 64, NB), F32), S((8, 16, NB), F32)),
        in_specs=[any_] * 6,
        out_specs=(any_, any_, vm, vm, vm, vm),
        scratch_shapes=scratch,
        compiler_params=pltpu.CompilerParams(collective_id=0, has_side_effects=True, vmem_limit_bytes=62 << 20),
        cost_estimate=pl.CostEstimate(flops=8 << 30, bytes_accessed=12 << 20, transcendentals=8 << 20),
        name="monarch_layer",
    )(tokens.transpose(1, 0, 2), cotangent.transpose(1, 0, 2), left_up, right_up, left_out, right_out)
    return out.transpose(1, 0, 2), tg.transpose(1, 0, 2), gl, gr, glo, gr2


def solution(mesh):
    wide, narrow = P("dp", "feat", None), P("feat", "dp", None)
    return jax.shard_map(
        on_device,
        mesh=mesh,
        in_specs=(wide, wide, narrow, narrow, narrow, narrow),
        out_specs=(wide, wide, narrow, narrow, narrow, narrow),
        check_vma=False,
    )
```

```python
import functools

import jax
import jax.numpy as jnp
from jax import lax
from jax.experimental import pallas as pl
from jax.experimental.pallas import tpu as pltpu
from jax.sharding import PartitionSpec as P

MESH = pl.DeviceIdType.MESH
BF = jnp.bfloat16
F32 = jnp.float32
NB = 128
EX = 512
T = 1024
TT = 256
NF = 16
ND = 8
NX = 4
QS = 4
NT = (((1,), (1,)), ((), ()))


def dot(a, b):
    return jnp.dot(a, b, preferred_element_type=F32)


def dot_nt(a, b):
    return lax.dot_general(a, b, NT, preferred_element_type=F32)


def gelu_parts(v):
    bell = jnp.exp2(v * v * (-0.7213475204444817)) * 0.3989422804014327
    t = 1.0 / (1.0 + 0.2316419 * jnp.abs(v))
    poly = 1.330274429 * t - 1.821255978
    poly = poly * t + 1.781477937
    poly = poly * t - 0.356563782
    poly = poly * t + 0.319381530
    tail = bell * (poly * t)
    phi = jnp.where(v >= 0, 1.0 - tail, tail)
    return v * phi, phi + v * bell


def layer(tok_h, cot_h, l_h, r_h, lo_h, r2_h,
          nat_o, nat_t, gl_o, gr_o, glo_o, gr2_o,
          tok, cot, lg, rg, log_, r2g,
          a1, a3, a2, a4, s1, s3, s2, s4, z1, z3,
          xc, fc, rt, lot, act, bp, zf, zb,
          gr_s, glo_s, gl_s, gr2_s, gr_r, glo_r, gl_r, gr2_r,
          gr_y, glo_y, gr2_y, gr_yr, glo_yr, gr2_yr, zr, zo,
          in_sem, own_sem,
          agy_s, agy_r, agx_s, agx_r, aa_s, aa_r, rx_s, rx_r, ry_s, ry_r):
    dp = lax.axis_index("dp")
    me = lax.axis_index("feat")
    x, yh = lax.div(dp, 2), lax.rem(dp, 2)
    partner = (x * 2 + (1 - yh), me)

    def xpeer(i):
        return (lax.rem(x + i, NX) * 2 + yh, me)

    def fpeer(i):
        return lax.rem(me + i, NF)

    ins = [pltpu.make_async_copy(tok_h, nat_o, in_sem.at[0]), pltpu.make_async_copy(cot_h, nat_t, in_sem.at[1])]
    for c in ins:
        c.start()
    facs = [(l_h, lg, 16), (r2_h, r2g, 16), (r_h, rg, 16), (lo_h, log_, 64)]
    own = [pltpu.make_async_copy(sh, g.at[:, pl.ds(pl.multiple_of(dp * n, n), n), :], own_sem.at[k])
           for k, (sh, g, n) in enumerate(facs)]
    for c in own:
        c.start()

    barrier = pltpu.get_barrier_semaphore()

    def dpeer(i):
        return (lax.rem(dp + i, ND), me)

    def greet(i, _):
        pl.semaphore_signal(barrier, inc=1, device_id=(dp, fpeer(i)), device_id_type=MESH)
        return 0

    lax.fori_loop(1, NF, greet, 0)

    def greet_group(i, _):
        pl.semaphore_signal(barrier, inc=1, device_id=dpeer(i), device_id_type=MESH)
        return 0

    lax.fori_loop(1, ND, greet_group, 0)
    pl.semaphore_wait(barrier, NF - 1 + ND - 1)

    def remote(src, dst, ss, rs, dev):
        return pltpu.make_async_remote_copy(src_ref=src, dst_ref=dst, send_sem=ss, recv_sem=rs,
                                            device_id=dev, device_id_type=MESH)

    def await_bytes(ref, sem):
        pltpu.make_async_copy(ref, ref, sem).wait()

    def share_y(k):
        sh, g, n = facs[k]
        mine = g.at[:, pl.ds(pl.multiple_of(dp * n, n), n), :]
        remote(sh, mine, agy_s.at[k], agy_r.at[k], partner).start()

    def share_x(k):
        sh, g, n = facs[k]
        mine = g.at[:, pl.ds(pl.multiple_of(dp * n, n), n), :]
        for i in range(1, NX):
            remote(sh, mine, agx_s.at[k], agx_r.at[k], xpeer(i)).start()

    def forward_shard(k):
        sh, g, n = facs[k]
        theirs = g.at[:, pl.ds(pl.multiple_of(partner[0] * n, n), n), :]
        await_bytes(theirs, agy_r.at[k])
        for i in range(1, NX):
            remote(theirs, theirs, agx_s.at[k], agx_r.at[k], xpeer(i)).start()

    def gathered(k):
        sh, g, n = facs[k]
        own[k].wait()
        await_bytes(g.at[:, pl.ds(0, (7 if k < 2 else 6) * n), :], agx_r.at[k])

    def share_all(k):
        sh, g, n = facs[k]
        mine = g.at[:, pl.ds(pl.multiple_of(dp * n, n), n), :]

        def go(i, _):
            remote(sh, mine, agx_s.at[k], agx_r.at[k], dpeer(i)).start()
            return 0

        lax.fori_loop(1, ND, go, 0)

    share_all(0)
    share_all(1)
    share_y(2)
    share_y(3)

    def relay(nat, dst):
        def one(j, _):
            rows = pl.ds(pl.multiple_of(j * 128, 128), 128)
            zr[...] = nat[rows].astype(F32).reshape(1024, 128)
            for a in range(8):
                dst[a, rows, :] = zr[pl.ds(a, 128, stride=8), :].astype(BF)
            return 0

        lax.fori_loop(0, T // 128, one, 0)

    ins[0].wait()
    share_x(2)
    share_x(3)
    relay(nat_o, tok)

    def spread(z, a, res, t0):
        for h in range(TT // 128):
            z[t0 // 128 + h, pl.ds(a, NB, stride=8), :] = res[:, h * 128:(h + 1) * 128]

    def send_pair(z, abuf, sbuf, kind, q):
        def one(i, _):
            p = fpeer(i)
            rows = pl.ds(pl.multiple_of(p * 16, 16), 16)
            for tt in range(T // 128):
                piece = z[tt, pl.ds(pl.multiple_of(p * 64 + q * 16, 16), 16), :].astype(BF)
                abuf[q, rows, tt * 128:(tt + 1) * 128] = piece
            return 0

        lax.fori_loop(0, NF, one, 0)
        ship(abuf, sbuf, kind, q)

    def ship(abuf, sbuf, kind, q):
        mine = pl.ds(pl.multiple_of(me * 16, 16), 16)

        def go(i, _):
            p = fpeer(i)
            rows = pl.ds(pl.multiple_of(p * 16, 16), 16)
            remote(abuf.at[q, rows, :], sbuf.at[q, mine, :], aa_s.at[kind, q], aa_r.at[kind, q], (dp, p)).start()
            return 0

        lax.fori_loop(1, NF, go, 0)
        sbuf[q, mine, :] = abuf[q, mine, :]

    def arrived(sbuf, kind, q):
        await_bytes(sbuf.at[q, pl.ds(0, 240), :], aa_r.at[kind, q])

    gathered(0)
    for a in range(8):
        lt = lg[a].astype(F32).T.astype(BF)
        for t0 in range(0, T, TT):
            spread(z1, a, dot_nt(lt, tok[a, t0:t0 + TT, :]), t0)
    send_pair(z1, a1, s1, 0, 0)
    ins[1].wait()
    relay(nat_t, cot)
    gathered(1)
    for f in range(8):
        for t0 in range(0, T, TT):
            spread(z3, f, dot_nt(r2g[f], cot[f, t0:t0 + TT, :]), t0)
    send_pair(z3, a3, s3, 1, 0)
    forward_shard(2)
    forward_shard(3)

    def rest(q, _):
        send_pair(z1, a1, s1, 0, q)
        send_pair(z3, a3, s3, 1, q)
        return 0

    lax.fori_loop(1, QS, rest, 0)
    gathered(2)
    gathered(3)

    def sum_x(src, dst, n, lead, sem):
        for i in range(1, NX):
            to = lax.rem(x + i, NX)
            remote(src.at[lead, pl.ds(pl.multiple_of(to * 2 * n, 2 * n), 2 * n), :], dst.at[i - 1, lead],
                   rx_s.at[sem], rx_r.at[sem], xpeer(i)).start()

    scale = 1.0 / jnp.sqrt(F32(8192.0))

    def sum_y(src, dst, ybuf, yrecv, res, n, lead, sem):
        await_bytes(dst.at[:, lead], rx_r.at[sem])
        for half in range(2):
            total = src[lead, pl.ds(pl.multiple_of(x * 2 * n + half * n, n), n), :].astype(F32)
            for i in range(NX - 1):
                total += dst[i, lead, half * n:(half + 1) * n, :].astype(F32)

            @pl.when(yh == half)
            def _():
                res[lead] = total

            @pl.when(yh != half)
            def _():
                ybuf[lead] = total.astype(BF)

        remote(ybuf.at[lead], yrecv.at[lead], ry_s.at[sem], ry_r.at[sem], partner).start()

    def finish(yrecv, res, lead, sem):
        await_bytes(yrecv.at[lead], ry_r.at[sem])
        res[lead] = (res[lead] + yrecv[lead].astype(F32)) * scale

    def pair(q, _):
        arrived(s1, 0, q)
        arrived(s3, 1, q)
        for t0 in range(0, T, TT):
            for src, dst in ((s1, xc), (s3, fc)):
                slab = src[q, :, t0:t0 + TT].astype(F32).reshape(NF, 2, 8, TT)
                for h in range(2):
                    dst[h, :, t0:t0 + TT] = slab[:, h].reshape(NB, TT).astype(BF)

        def block(h, _):
            c = q * 2 + h
            rt[...] = rg[c].astype(F32).T.astype(BF)
            lot[...] = log_[c].astype(F32).T.astype(BF)

            def tile(j, _):
                cols = pl.ds(pl.multiple_of(j * TT, TT), TT)
                active, slope = gelu_parts(dot(rt[...], xc[h, :, cols]))
                active = active.astype(BF)
                act[:, cols] = active
                back = (dot(log_[c], fc[h, :, cols]) * slope).astype(BF)
                bp[:, cols] = back
                zf[h, :, cols] = dot(lot[...], active)
                zb[h, :, cols] = dot(rg[c], back)
                return 0

            lax.fori_loop(0, T // TT, tile, 0)
            glo_s[c] = dot_nt(act[...], fc[h]).astype(BF)
            gr_s[c] = dot_nt(xc[h], bp[...]).astype(BF)
            return 0

        lax.fori_loop(0, 2, block, 0)

        for z, abuf, sbuf, kind in ((zf, a2, s2, 2), (zb, a4, s4, 3)):
            def pack(p, _):
                rows = pl.ds(pl.multiple_of(p * 8, 8), 8)
                both = jnp.concatenate([z[0, rows, :], z[1, rows, :]], axis=0)
                abuf[q, pl.ds(pl.multiple_of(p * 16, 16), 16), :] = both.astype(BF)
                return 0

            lax.fori_loop(0, NF, pack, 0)
            if kind == 2:
                ship(abuf, sbuf, kind, q)

        lead = pl.ds(q * 2, 2)
        sum_x(gr_s, gr_r, 16, lead, q)
        sum_x(glo_s, glo_r, 64, lead, QS + q)

        @pl.when(q > 0)
        def _():
            before = pl.ds(q * 2 - 2, 2)
            sum_y(gr_s, gr_r, gr_y, gr_yr, gr_o, 16, before, q - 1)
            sum_y(glo_s, glo_r, glo_y, glo_yr, glo_o, 64, before, QS + q - 1)

        return 0

    lax.fori_loop(0, QS, pair, 0)

    def ship_back(q, _):
        ship(a4, s4, 3, q)
        return 0

    lax.fori_loop(0, QS, ship_back, 0)

    def gather_rows(sbuf, kind, z, first, last):
        def one_q(q, _):
            arrived(sbuf, kind, q)

            def one_k(k, _):
                rows = pl.ds(pl.multiple_of(k * 16, 16), 16)
                for tt in range(T // 128):
                    slab = sbuf[q, rows, tt * 128:(tt + 1) * 128].astype(F32)
                    for h in range(2):
                        z[tt, pl.ds(k * 8 + q * 2 + h, 8, stride=NB), :] = slab[h * 8:(h + 1) * 8]
                return 0

            lax.fori_loop(0, NF, one_k, 0)
            return 0

        lax.fori_loop(first, last, one_q, 0)

    eye = (lax.broadcasted_iota(jnp.int32, (TT, TT), 0) == lax.broadcasted_iota(jnp.int32, (TT, TT), 1)).astype(BF)

    def block_rows(z, f):
        rows = pl.ds(pl.multiple_of(f * NB, NB), NB)
        return [z[tt, rows, :].astype(BF) for tt in range(T // 128)]

    gather_rows(s2, 2, z1, 0, QS)

    def last_pair():
        lead = pl.ds(QS * 2 - 2, 2)
        sum_y(gr_s, gr_r, gr_y, gr_yr, gr_o, 16, lead, QS - 1)
        sum_y(glo_s, glo_r, glo_y, glo_yr, glo_o, 64, lead, 2 * QS - 1)

    def f_block(f, _):
        y = jnp.concatenate(block_rows(z1, f), axis=1)
        gr2_s[f] = dot(y, cot[f]).astype(BF)
        return 0

    lax.fori_loop(0, 8, f_block, 0)
    every = pl.ds(0, 8)
    sum_x(gr2_s, gr2_r, 16, every, 2 * QS)

    def write_out(z, tile_of, nat):
        def one(j, _):
            for f in range(8):
                pair_of = [z[j * 2 + h, f * NB:(f + 1) * NB, :].astype(BF) for h in range(TT // 128)]
                yt = dot_nt(eye, jnp.concatenate(pair_of, axis=1)).astype(BF)
                zo[pl.ds(f, TT, stride=8), :] = tile_of(yt, f)
            rows = pl.ds(pl.multiple_of(j * TT, TT), TT)
            nat[rows] = zo[...].reshape(TT, 8, NB).astype(BF)
            return 0

        lax.fori_loop(0, T // TT, one, 0)

    write_out(z1, lambda yt, f: dot(yt, r2g[f]), nat_o)
    gather_rows(s4, 3, z3, 0, QS - 1)
    last_pair()
    sum_y(gr2_s, gr2_r, gr2_y, gr2_yr, gr2_o, 16, every, 2 * QS)
    gather_rows(s4, 3, z3, QS - 1, QS)

    def a_grad(a, _):
        m = jnp.concatenate(block_rows(z3, a), axis=1)
        gl_s[a] = dot(m, tok[a]).T.astype(BF)
        return 0

    lax.fori_loop(0, 8, a_grad, 0)

    def give(i, _):
        to, g = dpeer(i)
        remote(gl_s.at[:, pl.ds(pl.multiple_of(to * 16, 16), 16), :], gl_r.at[i - 1],
               rx_s.at[2 * QS + 1], rx_r.at[2 * QS + 1], (to, g)).start()
        return 0

    lax.fori_loop(1, ND, give, 0)
    write_out(z3, lambda yt, a: dot_nt(yt, lg[a]), nat_t)

    def fin(q, _):
        lead = pl.ds(q * 2, 2)
        finish(gr_yr, gr_o, lead, q)
        finish(glo_yr, glo_o, lead, QS + q)
        return 0

    lax.fori_loop(0, QS, fin, 0)
    finish(gr2_yr, gr2_o, every, 2 * QS)
    await_bytes(gl_r, rx_r.at[2 * QS + 1])
    total = gl_s[:, pl.ds(pl.multiple_of(dp * 16, 16), 16), :].astype(F32)
    for i in range(ND - 1):
        total += gl_r[i].astype(F32)
    gl_o[...] = total * scale

    for k, (sh, g, n) in enumerate(facs):
        if k >= 2:
            await_bytes(g.at[:, pl.ds(0, n), :], agy_s.at[k])
        await_bytes(g.at[:, pl.ds(0, (7 if k < 2 else 6) * n), :], agx_s.at[k])

    def drain(q, _):
        for kind, buf in enumerate((a1, a3, a2, a4)):
            await_bytes(buf.at[q, pl.ds(0, 240), :], aa_s.at[kind, q])
        lead = pl.ds(q * 2, 2)
        await_bytes(gr_r.at[:, lead], rx_s.at[q])
        await_bytes(glo_r.at[:, lead], rx_s.at[QS + q])
        await_bytes(gr_yr.at[lead], ry_s.at[q])
        await_bytes(glo_yr.at[lead], ry_s.at[QS + q])
        return 0

    lax.fori_loop(0, QS, drain, 0)
    await_bytes(gr2_r, rx_s.at[2 * QS])
    await_bytes(gl_r, rx_s.at[2 * QS + 1])
    await_bytes(gr2_yr, ry_s.at[2 * QS])


def copy_all(*refs):
    copies = [pltpu.make_async_copy(refs[i], refs[6 + i], refs[12].at[i]) for i in range(6)]
    for c in copies:
        c.start()
    for c in copies:
        c.wait()


def on_device(tokens, cotangent, left_up, right_up, left_out, right_out):
    any_, vm = pl.BlockSpec(memory_space=pl.ANY), pl.BlockSpec(memory_space=pltpu.VMEM)
    V, D = pltpu.VMEM, pltpu.SemaphoreType.DMA
    slab = V((QS, NF * 16, T), BF)
    scratch = [
        V((8, T, NB), BF), V((8, T, NB), BF),
        V((8, NB, NB), BF), V((8, NB, EX), BF), V((8, EX, NB), BF), V((8, NB, NB), BF),
        slab, slab, slab, slab, slab, slab, slab, slab,
        V((T // 128, 1024, 128), F32), V((T // 128, 1024, 128), F32),
        V((2, NB, T), BF), V((2, NB, T), BF), V((EX, NB), BF), V((NB, EX), BF),
        V((EX, T), BF), V((EX, T), BF), V((2, NB, T), F32), V((2, NB, T), F32),
        V((8, NB, EX), BF), V((8, EX, NB), BF), V((8, NB, NB), BF), V((8, NB, NB), BF),
        V((3, 8, 32, EX), BF), V((3, 8, 128, NB), BF), V((7, 8, 16, NB), BF), V((3, 8, 32, NB), BF),
        V((8, 16, EX), BF), V((8, 64, NB), BF), V((8, 16, NB), BF),
        V((8, 16, EX), BF), V((8, 64, NB), BF), V((8, 16, NB), BF),
        V((1024, 128), F32), V((TT * 8, NB), F32),
        D((2,)), D((4,)),
        D((4,)), D((4,)), D((4,)), D((4,)), D((4, QS)), D((4, QS)),
        D((2 * QS + 2,)), D((2 * QS + 2,)), D((2 * QS + 1,)), D((2 * QS + 1,)),
    ]
    S = jax.ShapeDtypeStruct
    results = pl.pallas_call(
        layer,
        out_shape=(V((T, 8, NB), BF), V((T, 8, NB), BF), V((8, 16, NB), F32), V((8, 16, EX), F32),
                   V((8, 64, NB), F32), V((8, 16, NB), F32)),
        in_specs=[any_] * 6,
        out_specs=(vm,) * 6,
        scratch_shapes=scratch,
        compiler_params=pltpu.CompilerParams(collective_id=0, has_side_effects=True, vmem_limit_bytes=52 << 20),
        cost_estimate=pl.CostEstimate(flops=8 << 30, bytes_accessed=12 << 20, transcendentals=8 << 20),
        name="monarch_layer",
    )(tokens, cotangent, left_up, right_up, left_out, right_out)
    return pl.pallas_call(
        copy_all,
        out_shape=tuple(S(r.shape, r.dtype) for r in results),
        in_specs=[vm] * 6,
        out_specs=(any_,) * 6,
        scratch_shapes=[D((6,))],
        compiler_params=pltpu.CompilerParams(vmem_limit_bytes=1 << 20),
        name="copy_results",
    )(*[pltpu.with_memory_space_constraint(r, V) for r in results])


def solution(mesh):
    wide, narrow = P("dp", "feat", None), P("feat", "dp", None)
    return jax.shard_map(
        on_device,
        mesh=mesh,
        in_specs=(wide, wide, narrow, narrow, narrow, narrow),
        out_specs=(wide, wide, narrow, narrow, narrow, narrow),
        check_vma=False,
    )
```

```python
import functools

import jax
import jax.numpy as jnp
from jax import lax
from jax.experimental import pallas as pl
from jax.experimental.pallas import tpu as pltpu
from jax.sharding import PartitionSpec as P

MESH = pl.DeviceIdType.MESH
BF = jnp.bfloat16
F32 = jnp.float32
NB = 128
EX = 512
T = 1024
TT = 256
NF = 16
ND = 8
NX = 4
QS = 4
NT = (((1,), (1,)), ((), ()))


def dot(a, b):
    return jnp.dot(a, b, preferred_element_type=F32)


def dot_nt(a, b):
    return lax.dot_general(a, b, NT, preferred_element_type=F32)


def gelu_parts(v):
    bell = jnp.exp2(v * v * (-0.7213475204444817)) * 0.3989422804014327
    t = 1.0 / (1.0 + 0.2316419 * jnp.abs(v))
    poly = 1.330274429 * t - 1.821255978
    poly = poly * t + 1.781477937
    poly = poly * t - 0.356563782
    poly = poly * t + 0.319381530
    tail = bell * (poly * t)
    phi = jnp.where(v >= 0, 1.0 - tail, tail)
    return v * phi, phi + v * bell


def layer(tok_h, cot_h, l_h, r_h, lo_h, r2_h,
          nat_o, nat_t, gl_o, gr_o, glo_o, gr2_o,
          tok, cot, lg, rg, log_, r2g,
          a1, a3, a2, a4, s1, s3, s2, s4, z1, z3,
          xc, fc, rt, lot, act, bp, zf, zb,
          gr_s, glo_s, gl_s, gr2_s, gr_r, glo_r, gl_r, gr2_r,
          gr_y, glo_y, gr2_y, gr_yr, glo_yr, gr2_yr, zr, zo, gl_acc,
          in_sem, own_sem,
          agy_s, agy_r, agx_s, agx_r, aa_s, aa_r, rx_s, rx_r, ry_s, ry_r):
    dp = lax.axis_index("dp")
    me = lax.axis_index("feat")
    x, yh = lax.div(dp, 2), lax.rem(dp, 2)
    partner = (x * 2 + (1 - yh), me)

    def xpeer(i):
        return (lax.rem(x + i, NX) * 2 + yh, me)

    def fpeer(i):
        return lax.rem(me + i, NF)

    ins = [pltpu.make_async_copy(tok_h, nat_o, in_sem.at[0]), pltpu.make_async_copy(cot_h, nat_t, in_sem.at[1])]
    for c in ins:
        c.start()
    facs = [(l_h, lg, 16), (r2_h, r2g, 16), (r_h, rg, 16), (lo_h, log_, 64)]
    own = [pltpu.make_async_copy(sh, g.at[:, pl.ds(pl.multiple_of(dp * n, n), n), :], own_sem.at[k])
           for k, (sh, g, n) in enumerate(facs)]
    for c in own:
        c.start()

    barrier = pltpu.get_barrier_semaphore()

    def dpeer(i):
        return (lax.rem(dp + i, ND), me)

    def greet(i, _):
        pl.semaphore_signal(barrier, inc=1, device_id=(dp, fpeer(i)), device_id_type=MESH)
        return 0

    lax.fori_loop(1, NF, greet, 0)

    def greet_group(i, _):
        pl.semaphore_signal(barrier, inc=1, device_id=dpeer(i), device_id_type=MESH)
        return 0

    lax.fori_loop(1, ND, greet_group, 0)
    pl.semaphore_wait(barrier, NF - 1 + ND - 1)

    def remote(src, dst, ss, rs, dev):
        return pltpu.make_async_remote_copy(src_ref=src, dst_ref=dst, send_sem=ss, recv_sem=rs,
                                            device_id=dev, device_id_type=MESH)

    def await_bytes(ref, sem):
        pltpu.make_async_copy(ref, ref, sem).wait()

    def share_y(k):
        sh, g, n = facs[k]
        mine = g.at[:, pl.ds(pl.multiple_of(dp * n, n), n), :]
        own[k].wait()
        remote(mine, mine, agy_s.at[k], agy_r.at[k], partner).start()

    def share_x(k):
        sh, g, n = facs[k]
        mine = g.at[:, pl.ds(pl.multiple_of(dp * n, n), n), :]
        for i in range(1, NX):
            remote(mine, mine, agx_s.at[k], agx_r.at[k], xpeer(i)).start()

    def forward_shard(k):
        sh, g, n = facs[k]
        theirs = g.at[:, pl.ds(pl.multiple_of(partner[0] * n, n), n), :]
        await_bytes(theirs, agy_r.at[k])
        for i in range(1, NX):
            remote(theirs, theirs, agx_s.at[k], agx_r.at[k], xpeer(i)).start()

    def gathered(k):
        sh, g, n = facs[k]
        await_bytes(g.at[:, pl.ds(0, 6 * n), :], agx_r.at[k])

    share_y(0)
    share_x(0)

    def relay(nat, dst):
        def one(j, _):
            rows = pl.ds(pl.multiple_of(j * 128, 128), 128)
            zr[...] = nat[rows].astype(F32).reshape(1024, 128)
            for a in range(8):
                dst[a, rows, :] = zr[pl.ds(a, 128, stride=8), :].astype(BF)
            return 0

        lax.fori_loop(0, T // 128, one, 0)

    forward_shard(0)
    for k in range(1, 4):
        share_y(k)
    share_x(1)
    ins[0].wait()
    relay(nat_o, tok)
    forward_shard(1)

    def spread(z, a, res, t0):
        for h in range(TT // 128):
            z[t0 // 128 + h, pl.ds(a, NB, stride=8), :] = res[:, h * 128:(h + 1) * 128]

    def send_pair(z, abuf, sbuf, kind, q):
        def one(i, _):
            p = fpeer(i)
            rows = pl.ds(pl.multiple_of(p * 16, 16), 16)
            for tt in range(T // 128):
                piece = z[tt, pl.ds(pl.multiple_of(p * 64 + q * 16, 16), 16), :].astype(BF)
                abuf[q, rows, tt * 128:(tt + 1) * 128] = piece
            return 0

        lax.fori_loop(0, NF, one, 0)
        ship(abuf, sbuf, kind, q)

    def ship(abuf, sbuf, kind, q):
        mine = pl.ds(pl.multiple_of(me * 16, 16), 16)

        def go(i, _):
            p = fpeer(i)
            rows = pl.ds(pl.multiple_of(p * 16, 16), 16)
            remote(abuf.at[q, rows, :], sbuf.at[q, mine, :], aa_s.at[kind, q], aa_r.at[kind, q], (dp, p)).start()
            return 0

        lax.fori_loop(1, NF, go, 0)
        sbuf[q, mine, :] = abuf[q, mine, :]

    def arrived(sbuf, kind, q):
        await_bytes(sbuf.at[q, pl.ds(0, 240), :], aa_r.at[kind, q])

    gathered(0)
    for a in range(8):
        lt = lg[a].astype(F32).T.astype(BF)
        for t0 in range(0, T, TT):
            spread(z1, a, dot_nt(lt, tok[a, t0:t0 + TT, :]), t0)
    send_pair(z1, a1, s1, 0, 0)
    share_x(2)
    share_x(3)
    send_pair(z1, a1, s1, 0, 1)
    ins[1].wait()
    relay(nat_t, cot)
    gathered(1)
    for f in range(8):
        for t0 in range(0, T, TT):
            spread(z3, f, dot_nt(r2g[f], cot[f, t0:t0 + TT, :]), t0)
    send_pair(z3, a3, s3, 1, 0)
    forward_shard(2)
    forward_shard(3)
    send_pair(z3, a3, s3, 1, 1)

    def rest(q, _):
        send_pair(z1, a1, s1, 0, q)
        send_pair(z3, a3, s3, 1, q)
        return 0

    lax.fori_loop(2, QS, rest, 0)
    gathered(2)
    gathered(3)

    def sum_x(src, dst, n, lead, sem):
        for i in range(1, NX):
            to = lax.rem(x + i, NX)
            remote(src.at[lead, pl.ds(pl.multiple_of(to * 2 * n, 2 * n), 2 * n), :], dst.at[i - 1, lead],
                   rx_s.at[sem], rx_r.at[sem], xpeer(i)).start()

    scale = 1.0 / jnp.sqrt(F32(8192.0))

    def sum_y(src, dst, ybuf, res, n, lead, sem):
        await_bytes(dst.at[:, lead], rx_r.at[sem])
        for half in range(2):
            total = src[lead, pl.ds(pl.multiple_of(x * 2 * n + half * n, n), n), :].astype(F32)
            for i in range(NX - 1):
                total += dst[i, lead, half * n:(half + 1) * n, :].astype(F32)

            @pl.when(yh == half)
            def _():
                res[lead] = total

            @pl.when(yh != half)
            def _():
                ybuf[lead] = total.astype(BF)

    def send_y(ybuf, yrecv, lead, sem):
        remote(ybuf.at[lead], yrecv.at[lead], ry_s.at[sem], ry_r.at[sem], partner).start()

    def finish(yrecv, res, lead, sem):
        await_bytes(yrecv.at[lead], ry_r.at[sem])
        res[lead] = (res[lead] + yrecv[lead].astype(F32)) * scale

    def pair(q, _):
        arrived(s1, 0, q)
        arrived(s3, 1, q)
        for t0 in range(0, T, TT):
            for src, dst in ((s1, xc), (s3, fc)):
                slab = src[q, :, t0:t0 + TT].astype(F32).reshape(NF, 2, 8, TT)
                for h in range(2):
                    dst[h, :, t0:t0 + TT] = slab[:, h].reshape(NB, TT).astype(BF)

        def block(h, _):
            c = q * 2 + h
            rt[...] = rg[c].astype(F32).T.astype(BF)
            lot[...] = log_[c].astype(F32).T.astype(BF)

            def tile(j, _):
                cols = pl.ds(pl.multiple_of(j * TT, TT), TT)
                active, slope = gelu_parts(dot(rt[...], xc[h, :, cols]))
                active = active.astype(BF)
                act[:, cols] = active
                back = (dot(log_[c], fc[h, :, cols]) * slope).astype(BF)
                bp[:, cols] = back
                zf[h, :, cols] = dot(lot[...], active)
                zb[h, :, cols] = dot(rg[c], back)
                return 0

            lax.fori_loop(0, T // TT, tile, 0)
            glo_s[c] = dot_nt(act[...], fc[h]).astype(BF)
            gr_s[c] = dot_nt(xc[h], bp[...]).astype(BF)
            return 0

        lax.fori_loop(0, 2, block, 0)

        for z, abuf, sbuf, kind in ((zf, a2, s2, 2), (zb, a4, s4, 3)):
            def pack(p, _):
                rows = pl.ds(pl.multiple_of(p * 8, 8), 8)
                both = jnp.concatenate([z[0, rows, :], z[1, rows, :]], axis=0)
                abuf[q, pl.ds(pl.multiple_of(p * 16, 16), 16), :] = both.astype(BF)
                return 0

            lax.fori_loop(0, NF, pack, 0)
            if kind == 2:
                ship(abuf, sbuf, kind, q)

        lead = pl.ds(q * 2, 2)
        sum_x(gr_s, gr_r, 16, lead, q)
        sum_x(glo_s, glo_r, 64, lead, QS + q)

        @pl.when(q > 0)
        def _():
            before = pl.ds(q * 2 - 2, 2)
            sum_y(gr_s, gr_r, gr_y, gr_o, 16, before, q - 1)
            sum_y(glo_s, glo_r, glo_y, glo_o, 64, before, QS + q - 1)

        return 0

    lax.fori_loop(0, QS, pair, 0)

    def quarter(j):
        return pl.ds(pl.multiple_of(j * TT, TT), TT)

    def ship_back(j, _):
        mine = pl.ds(pl.multiple_of(me * 16, 16), 16)

        def go(i, _):
            p = fpeer(i)
            rows = pl.ds(pl.multiple_of(p * 16, 16), 16)
            remote(a4.at[:, rows, quarter(j)], s4.at[:, mine, quarter(j)], aa_s.at[3, j], aa_r.at[3, j], (dp, p)).start()
            return 0

        lax.fori_loop(1, NF, go, 0)
        s4[:, mine, quarter(j)] = a4[:, mine, quarter(j)]
        return 0

    lax.fori_loop(0, T // TT, ship_back, 0)

    def send_pair_y(q, _):
        lead = pl.ds(q * 2, 2)
        send_y(gr_y, gr_yr, lead, q)
        send_y(glo_y, glo_yr, lead, QS + q)
        return 0

    lax.fori_loop(0, QS - 1, send_pair_y, 0)

    def gather_rows(sbuf, z, first, count):
        def one_q(q, _):
            def one_k(k, _):
                rows = pl.ds(pl.multiple_of(k * 16, 16), 16)
                for i in range(count):
                    tt = first + i
                    slab = sbuf[q, rows, pl.ds(pl.multiple_of(tt * 128, 128), 128)].astype(F32)
                    for h in range(2):
                        z[tt, pl.ds(k * 8 + q * 2 + h, 8, stride=NB), :] = slab[h * 8:(h + 1) * 8]
                return 0

            lax.fori_loop(0, NF, one_k, 0)
            return 0

        lax.fori_loop(0, QS, one_q, 0)

    eye = (lax.broadcasted_iota(jnp.int32, (TT, TT), 0) == lax.broadcasted_iota(jnp.int32, (TT, TT), 1)).astype(BF)

    def block_rows(z, f, first, count):
        rows = pl.ds(pl.multiple_of(f * NB, NB), NB)
        return jnp.concatenate([z[first + i, rows, :].astype(BF) for i in range(count)], axis=1)

    def folded_here(q, _):
        arrived(s2, 2, q)
        return 0

    lax.fori_loop(0, QS, folded_here, 0)
    gather_rows(s2, z1, 0, T // 128)

    def last_pair():
        lead = pl.ds(QS * 2 - 2, 2)
        sum_y(gr_s, gr_r, gr_y, gr_o, 16, lead, QS - 1)
        sum_y(glo_s, glo_r, glo_y, glo_o, 64, lead, 2 * QS - 1)
        send_pair_y(QS - 1, 0)

    def f_block(f, _):
        gr2_s[f] = dot(block_rows(z1, f, 0, T // 128), cot[f]).astype(BF)
        return 0

    lax.fori_loop(0, 8, f_block, 0)
    every = pl.ds(0, 8)
    sum_x(gr2_s, gr2_r, 16, every, 2 * QS)

    def write_tile(z, tile_of, nat, j):
        for f in range(8):
            yt = dot_nt(eye, block_rows(z, f, j * 2, 2)).astype(BF)
            zo[pl.ds(f, TT, stride=8), :] = tile_of(yt, f)
        nat[quarter(j)] = zo[...].reshape(TT, 8, NB).astype(BF)

    def out_tile(j, _):
        write_tile(z1, lambda yt, f: dot(yt, r2g[f]), nat_o, j)
        return 0

    lax.fori_loop(0, T // TT, out_tile, 0)
    last_pair()
    sum_y(gr2_s, gr2_r, gr2_y, gr2_o, 16, every, 2 * QS)
    send_y(gr2_y, gr2_yr, every, 2 * QS)

    def back_tile(j):
        write_tile(z3, lambda yt, a: dot_nt(yt, lg[a]), nat_t, j)

    for a in range(8):
        gl_acc[a] = jnp.zeros((NB, NB), F32)

    def a_stage(j, _):
        await_bytes(s4.at[:, pl.ds(0, 240), quarter(j)], aa_r.at[3, j])
        gather_rows(s4, z3, j * 2, 2)
        for a in range(8):
            gl_acc[a] += dot(block_rows(z3, a, j * 2, 2), tok[a, quarter(j), :])
        return 0

    def a_early(j, _):
        a_stage(j, 0)
        back_tile(j)
        return 0

    lax.fori_loop(0, T // TT - 1, a_early, 0)
    a_stage(T // TT - 1, 0)
    for a in range(8):
        gl_s[a] = gl_acc[a].T.astype(BF)

    def give(i, _):
        to, g = dpeer(i)
        remote(gl_s.at[:, pl.ds(pl.multiple_of(to * 16, 16), 16), :], gl_r.at[i - 1],
               rx_s.at[2 * QS + 1], rx_r.at[2 * QS + 1], (to, g)).start()
        return 0

    lax.fori_loop(1, ND, give, 0)
    back_tile(T // TT - 1)

    def fin(q, _):
        lead = pl.ds(q * 2, 2)
        finish(gr_yr, gr_o, lead, q)
        finish(glo_yr, glo_o, lead, QS + q)
        return 0

    lax.fori_loop(0, QS, fin, 0)
    finish(gr2_yr, gr2_o, every, 2 * QS)
    await_bytes(gl_r, rx_r.at[2 * QS + 1])
    total = gl_s[:, pl.ds(pl.multiple_of(dp * 16, 16), 16), :].astype(F32)
    for i in range(ND - 1):
        total += gl_r[i].astype(F32)
    gl_o[...] = total * scale

    for k, (sh, g, n) in enumerate(facs):
        await_bytes(g.at[:, pl.ds(0, n), :], agy_s.at[k])
        await_bytes(g.at[:, pl.ds(0, 6 * n), :], agx_s.at[k])

    def drain(q, _):
        for kind, buf in enumerate((a1, a3, a2)):
            await_bytes(buf.at[q, pl.ds(0, 240), :], aa_s.at[kind, q])
        await_bytes(a4.at[:, pl.ds(0, 240), quarter(q)], aa_s.at[3, q])
        lead = pl.ds(q * 2, 2)
        await_bytes(gr_r.at[:, lead], rx_s.at[q])
        await_bytes(glo_r.at[:, lead], rx_s.at[QS + q])
        await_bytes(gr_yr.at[lead], ry_s.at[q])
        await_bytes(glo_yr.at[lead], ry_s.at[QS + q])
        return 0

    lax.fori_loop(0, QS, drain, 0)
    await_bytes(gr2_r, rx_s.at[2 * QS])
    await_bytes(gl_r, rx_s.at[2 * QS + 1])
    await_bytes(gr2_yr, ry_s.at[2 * QS])


CUTS = (4, 4, 1, 1, 1, 1)


def copy_all(*refs):
    copies = []
    for i, cuts in enumerate(CUTS):
        n = refs[i].shape[0] // cuts
        for j in range(cuts):
            rows = pl.ds(j * n, n)
            copies.append(pltpu.make_async_copy(refs[i].at[rows], refs[6 + i].at[rows], refs[12].at[len(copies)]))
    for c in copies:
        c.start()
    for c in copies:
        c.wait()


def on_device(tokens, cotangent, left_up, right_up, left_out, right_out):
    any_, vm = pl.BlockSpec(memory_space=pl.ANY), pl.BlockSpec(memory_space=pltpu.VMEM)
    V, D = pltpu.VMEM, pltpu.SemaphoreType.DMA
    slab = V((QS, NF * 16, T), BF)
    scratch = [
        V((8, T, NB), BF), V((8, T, NB), BF),
        V((8, NB, NB), BF), V((8, NB, EX), BF), V((8, EX, NB), BF), V((8, NB, NB), BF),
        slab, slab, slab, slab, slab, slab, slab, slab,
        V((T // 128, 1024, 128), F32), V((T // 128, 1024, 128), F32),
        V((2, NB, T), BF), V((2, NB, T), BF), V((EX, NB), BF), V((NB, EX), BF),
        V((EX, T), BF), V((EX, T), BF), V((2, NB, T), F32), V((2, NB, T), F32),
        V((8, NB, EX), BF), V((8, EX, NB), BF), V((8, NB, NB), BF), V((8, NB, NB), BF),
        V((3, 8, 32, EX), BF), V((3, 8, 128, NB), BF), V((7, 8, 16, NB), BF), V((3, 8, 32, NB), BF),
        V((8, 16, EX), BF), V((8, 64, NB), BF), V((8, 16, NB), BF),
        V((8, 16, EX), BF), V((8, 64, NB), BF), V((8, 16, NB), BF),
        V((1024, 128), F32), V((TT * 8, NB), F32), V((8, NB, NB), F32),
        D((2,)), D((4,)),
        D((4,)), D((4,)), D((4,)), D((4,)), D((4, QS)), D((4, QS)),
        D((2 * QS + 2,)), D((2 * QS + 2,)), D((2 * QS + 1,)), D((2 * QS + 1,)),
    ]
    S = jax.ShapeDtypeStruct
    results = pl.pallas_call(
        layer,
        out_shape=(V((T, 8, NB), BF), V((T, 8, NB), BF), V((8, 16, NB), F32), V((8, 16, EX), F32),
                   V((8, 64, NB), F32), V((8, 16, NB), F32)),
        in_specs=[any_] * 6,
        out_specs=(vm,) * 6,
        scratch_shapes=scratch,
        compiler_params=pltpu.CompilerParams(collective_id=0, has_side_effects=True, vmem_limit_bytes=52 << 20),
        cost_estimate=pl.CostEstimate(flops=8 << 30, bytes_accessed=12 << 20, transcendentals=8 << 20),
        name="monarch_layer",
    )(tokens, cotangent, left_up, right_up, left_out, right_out)
    return pl.pallas_call(
        copy_all,
        out_shape=tuple(S(r.shape, r.dtype) for r in results),
        in_specs=[vm] * 6,
        out_specs=(any_,) * 6,
        scratch_shapes=[D((sum(CUTS),))],
        compiler_params=pltpu.CompilerParams(vmem_limit_bytes=1 << 20),
        name="copy_results",
    )(*[pltpu.with_memory_space_constraint(r, V) for r in results])


def solution(mesh):
    wide, narrow = P("dp", "feat", None), P("feat", "dp", None)
    return jax.shard_map(
        on_device,
        mesh=mesh,
        in_specs=(wide, wide, narrow, narrow, narrow, narrow),
        out_specs=(wide, wide, narrow, narrow, narrow, narrow),
        check_vma=False,
    )
```

```python
import functools

import jax
import jax.numpy as jnp
from jax import lax
from jax.experimental import pallas as pl
from jax.experimental.pallas import tpu as pltpu
from jax.sharding import PartitionSpec as P

MESH = pl.DeviceIdType.MESH
BF = jnp.bfloat16
F32 = jnp.float32
NB = 128
EX = 512
T = 1024
TT = 256
NF = 16
ND = 8
NX = 4
QS = 4
STEPS = ((1, 2, 0), (1, 2, 1), (1, 1, 0), (1, 3, 0), (1, 1, 1), (1, 3, 1), (1, 0, 0), (1, 0, 1),
         (0, 2, 0), (0, 2, 1), (0, 1, 0), (0, 3, 0), (0, 1, 1), (0, 3, 1), (0, 0, 1))
NT = (((1,), (1,)), ((), ()))


def dot(a, b):
    return jnp.dot(a, b, preferred_element_type=F32)


def dot_nt(a, b):
    return lax.dot_general(a, b, NT, preferred_element_type=F32)


def gelu_parts(v):
    bell = jnp.exp2(v * v * (-0.7213475204444817)) * 0.3989422804014327
    t = 1.0 / (1.0 + 0.2316419 * jnp.abs(v))
    poly = 1.330274429 * t - 1.821255978
    poly = poly * t + 1.781477937
    poly = poly * t - 0.356563782
    poly = poly * t + 0.319381530
    tail = bell * (poly * t)
    phi = jnp.where(v >= 0, 1.0 - tail, tail)
    return v * phi, phi + v * bell


def layer(tok_h, cot_h, l_h, r_h, lo_h, r2_h,
          nat_o, nat_t, gl_o, gr_o, glo_o, gr2_o,
          tok, cot, lg, rg, log_, r2g,
          a1, a3, a2, a4, s1, s3, s2, s4, z1, z3,
          xc, fc, rt, lot, act, bp, zf, zb,
          gr_s, glo_s, gl_s, gr2_s, gr_r, glo_r, gl_r, gr2_r,
          gr_y, glo_y, gr2_y, gr_yr, glo_yr, gr2_yr, zr, zo, gl_acc,
          in_sem, own_sem,
          agy_s, agy_r, agx_s, agx_r, aa_s, aa_r, rx_s, rx_r, ry_s, ry_r):
    dp = lax.axis_index("dp")
    me = lax.axis_index("feat")
    x, yh = lax.div(dp, 2), lax.rem(dp, 2)
    partner = (x * 2 + (1 - yh), me)

    def xpeer(i):
        return (lax.rem(x + i, NX) * 2 + yh, me)

    fy, fz, fc_ = lax.div(me, 8), lax.rem(lax.div(me, 2), 4), lax.rem(me, 2)

    def fpeer(step):
        dy, dz, dc = step
        return lax.rem(fy + dy, 2) * 8 + lax.rem(fz + dz, 4) * 2 + lax.rem(fc_ + dc, 2)

    ins = [pltpu.make_async_copy(tok_h, nat_o, in_sem.at[0]), pltpu.make_async_copy(cot_h, nat_t, in_sem.at[1])]
    for c in ins:
        c.start()
    facs = [(l_h, lg, 16), (r2_h, r2g, 16), (r_h, rg, 16), (lo_h, log_, 64)]
    own = [pltpu.make_async_copy(sh, g.at[:, pl.ds(pl.multiple_of(dp * n, n), n), :], own_sem.at[k])
           for k, (sh, g, n) in enumerate(facs)]
    for c in own:
        c.start()

    barrier = pltpu.get_barrier_semaphore()

    def dpeer(i):
        return (lax.rem(dp + i, ND), me)

    def greet(i, _):
        pl.semaphore_signal(barrier, inc=1, device_id=(dp, lax.rem(me + i, NF)), device_id_type=MESH)
        return 0

    lax.fori_loop(1, NF, greet, 0)

    def greet_group(i, _):
        pl.semaphore_signal(barrier, inc=1, device_id=dpeer(i), device_id_type=MESH)
        return 0

    lax.fori_loop(1, ND, greet_group, 0)
    pl.semaphore_wait(barrier, NF - 1 + ND - 1)

    def remote(src, dst, ss, rs, dev):
        return pltpu.make_async_remote_copy(src_ref=src, dst_ref=dst, send_sem=ss, recv_sem=rs,
                                            device_id=dev, device_id_type=MESH)

    def await_bytes(ref, sem):
        pltpu.make_async_copy(ref, ref, sem).wait()

    def share_y(k):
        sh, g, n = facs[k]
        mine = g.at[:, pl.ds(pl.multiple_of(dp * n, n), n), :]
        own[k].wait()
        remote(mine, mine, agy_s.at[k], agy_r.at[k], partner).start()

    def share_x(k):
        sh, g, n = facs[k]
        mine = g.at[:, pl.ds(pl.multiple_of(dp * n, n), n), :]
        for i in range(1, NX):
            remote(mine, mine, agx_s.at[k], agx_r.at[k], xpeer(i)).start()

    def forward_shard(k):
        sh, g, n = facs[k]
        theirs = g.at[:, pl.ds(pl.multiple_of(partner[0] * n, n), n), :]
        await_bytes(theirs, agy_r.at[k])
        for i in range(1, NX):
            remote(theirs, theirs, agx_s.at[k], agx_r.at[k], xpeer(i)).start()

    def gathered(k):
        sh, g, n = facs[k]
        await_bytes(g.at[:, pl.ds(0, 6 * n), :], agx_r.at[k])

    share_y(1)
    share_x(1)
    for k in (0, 2, 3):
        share_y(k)

    def relay(nat, dst):
        def one(j, _):
            rows = pl.ds(pl.multiple_of(j * 128, 128), 128)
            zr[...] = nat[rows].astype(F32).reshape(1024, 128)
            for a in range(8):
                dst[a, rows, :] = zr[pl.ds(a, 128, stride=8), :].astype(BF)
            return 0

        lax.fori_loop(0, T // 128, one, 0)

    forward_shard(1)
    share_x(0)
    ins[1].wait()
    relay(nat_t, cot)
    forward_shard(0)

    def spread(z, a, res, t0):
        for h in range(TT // 128):
            z[t0 // 128 + h, pl.ds(a, NB, stride=8), :] = res[:, h * 128:(h + 1) * 128]

    def send_pair(z, abuf, sbuf, kind, q, first=0, end=T // 128):
        def one(p, _):
            rows = pl.ds(pl.multiple_of(p * 16, 16), 16)
            for tt in range(first, end):
                piece = z[tt, pl.ds(pl.multiple_of(p * 64 + q * 16, 16), 16), :].astype(BF)
                abuf[q, rows, tt * 128:(tt + 1) * 128] = piece
            return 0

        lax.fori_loop(0, NF, one, 0)
        ship(abuf, sbuf, kind, q, pl.ds(first * 128, (end - first) * 128))

    def ship(abuf, sbuf, kind, q, cols=pl.ds(0, T)):
        mine = pl.ds(pl.multiple_of(me * 16, 16), 16)

        for step in STEPS:
            p = fpeer(step)
            rows = pl.ds(pl.multiple_of(p * 16, 16), 16)
            remote(abuf.at[q, rows, cols], sbuf.at[q, mine, cols], aa_s.at[kind, q], aa_r.at[kind, q], (dp, p)).start()
        sbuf[q, mine, cols] = abuf[q, mine, cols]

    def arrived(sbuf, kind, q):
        await_bytes(sbuf.at[q, pl.ds(0, 240), :], aa_r.at[kind, q])

    gathered(1)
    for first in (0, 4):
        for f in range(8):
            for t0 in range(first * 128, first * 128 + T // 2, TT):
                spread(z3, f, dot_nt(r2g[f], cot[f, t0:t0 + TT, :]), t0)
        send_pair(z3, a3, s3, 1, 0, first, first + 4)
    share_x(2)
    share_x(3)
    send_pair(z3, a3, s3, 1, 1)
    ins[0].wait()
    relay(nat_o, tok)
    gathered(0)
    for a in range(8):
        lt = lg[a].astype(F32).T.astype(BF)
        for t0 in range(0, T, TT):
            spread(z1, a, dot_nt(lt, tok[a, t0:t0 + TT, :]), t0)
    send_pair(z1, a1, s1, 0, 0)
    forward_shard(2)
    forward_shard(3)
    send_pair(z1, a1, s1, 0, 1)

    def rest(q, _):
        send_pair(z1, a1, s1, 0, q)
        send_pair(z3, a3, s3, 1, q)
        return 0

    lax.fori_loop(2, QS, rest, 0)
    gathered(2)
    gathered(3)

    def sum_x(src, dst, n, lead, sem):
        for i in range(1, NX):
            to = lax.rem(x + i, NX)
            remote(src.at[lead, pl.ds(pl.multiple_of(to * 2 * n, 2 * n), 2 * n), :], dst.at[i - 1, lead],
                   rx_s.at[sem], rx_r.at[sem], xpeer(i)).start()

    scale = 1.0 / jnp.sqrt(F32(8192.0))

    def sum_y(src, dst, ybuf, res, n, lead, sem):
        await_bytes(dst.at[:, lead], rx_r.at[sem])
        for half in range(2):
            total = src[lead, pl.ds(pl.multiple_of(x * 2 * n + half * n, n), n), :].astype(F32)
            for i in range(NX - 1):
                total += dst[i, lead, half * n:(half + 1) * n, :].astype(F32)

            @pl.when(yh == half)
            def _():
                res[lead] = total

            @pl.when(yh != half)
            def _():
                ybuf[lead] = total.astype(BF)

    def send_y(ybuf, yrecv, lead, sem):
        remote(ybuf.at[lead], yrecv.at[lead], ry_s.at[sem], ry_r.at[sem], partner).start()

    def finish(yrecv, res, lead, sem):
        await_bytes(yrecv.at[lead], ry_r.at[sem])
        res[lead] = (res[lead] + yrecv[lead].astype(F32)) * scale

    def pair(q, _):
        arrived(s1, 0, q)
        arrived(s3, 1, q)
        for t0 in range(0, T, TT):
            for src, dst in ((s1, xc), (s3, fc)):
                slab = src[q, :, t0:t0 + TT].astype(F32).reshape(NF, 2, 8, TT)
                for h in range(2):
                    dst[h, :, t0:t0 + TT] = slab[:, h].reshape(NB, TT).astype(BF)

        def block(h, _):
            c = q * 2 + h
            rt[...] = rg[c].astype(F32).T.astype(BF)
            lot[...] = log_[c].astype(F32).T.astype(BF)

            def tile(j, _):
                cols = pl.ds(pl.multiple_of(j * TT, TT), TT)
                active, slope = gelu_parts(dot(rt[...], xc[h, :, cols]))
                active = active.astype(BF)
                act[:, cols] = active
                back = (dot(log_[c], fc[h, :, cols]) * slope).astype(BF)
                bp[:, cols] = back
                zf[h, :, cols] = dot(lot[...], active)
                zb[h, :, cols] = dot(rg[c], back)
                return 0

            lax.fori_loop(0, T // TT, tile, 0)
            glo_s[c] = dot_nt(act[...], fc[h]).astype(BF)
            gr_s[c] = dot_nt(xc[h], bp[...]).astype(BF)
            return 0

        lax.fori_loop(0, 2, block, 0)

        for z, abuf, sbuf, kind in ((zf, a2, s2, 2), (zb, a4, s4, 3)):
            def pack(p, _):
                rows = pl.ds(pl.multiple_of(p * 8, 8), 8)
                both = jnp.concatenate([z[0, rows, :], z[1, rows, :]], axis=0)
                abuf[q, pl.ds(pl.multiple_of(p * 16, 16), 16), :] = both.astype(BF)
                return 0

            lax.fori_loop(0, NF, pack, 0)
            if kind == 2:
                ship(abuf, sbuf, kind, q)

        lead = pl.ds(q * 2, 2)
        sum_x(gr_s, gr_r, 16, lead, q)
        sum_x(glo_s, glo_r, 64, lead, QS + q)

        @pl.when(q > 0)
        def _():
            before = pl.ds(q * 2 - 2, 2)
            sum_y(gr_s, gr_r, gr_y, gr_o, 16, before, q - 1)
            sum_y(glo_s, glo_r, glo_y, glo_o, 64, before, QS + q - 1)

        return 0

    lax.fori_loop(0, QS, pair, 0)

    def quarter(j):
        return pl.ds(pl.multiple_of(j * TT, TT), TT)

    def ship_back(j, _):
        mine = pl.ds(pl.multiple_of(me * 16, 16), 16)

        for step in STEPS:
            p = fpeer(step)
            rows = pl.ds(pl.multiple_of(p * 16, 16), 16)
            remote(a4.at[:, rows, quarter(j)], s4.at[:, mine, quarter(j)], aa_s.at[3, j], aa_r.at[3, j], (dp, p)).start()
        s4[:, mine, quarter(j)] = a4[:, mine, quarter(j)]
        return 0

    lax.fori_loop(0, T // TT, ship_back, 0)

    def send_pair_y(q, _):
        lead = pl.ds(q * 2, 2)
        send_y(gr_y, gr_yr, lead, q)
        send_y(glo_y, glo_yr, lead, QS + q)
        return 0

    lax.fori_loop(0, QS - 1, send_pair_y, 0)

    def gather_rows(sbuf, z, first, count):
        def one_q(q, _):
            def one_k(k, _):
                rows = pl.ds(pl.multiple_of(k * 16, 16), 16)
                for i in range(count):
                    tt = first + i
                    slab = sbuf[q, rows, pl.ds(pl.multiple_of(tt * 128, 128), 128)].astype(F32)
                    for h in range(2):
                        z[tt, pl.ds(k * 8 + q * 2 + h, 8, stride=NB), :] = slab[h * 8:(h + 1) * 8]
                return 0

            lax.fori_loop(0, NF, one_k, 0)
            return 0

        lax.fori_loop(0, QS, one_q, 0)

    eye = (lax.broadcasted_iota(jnp.int32, (TT, TT), 0) == lax.broadcasted_iota(jnp.int32, (TT, TT), 1)).astype(BF)

    def block_rows(z, f, first, count):
        rows = pl.ds(pl.multiple_of(f * NB, NB), NB)
        return jnp.concatenate([z[first + i, rows, :].astype(BF) for i in range(count)], axis=1)

    def folded_here(q, _):
        arrived(s2, 2, q)
        return 0

    lax.fori_loop(0, QS, folded_here, 0)
    gather_rows(s2, z1, 0, T // 128)

    def last_pair():
        lead = pl.ds(QS * 2 - 2, 2)
        sum_y(gr_s, gr_r, gr_y, gr_o, 16, lead, QS - 1)
        sum_y(glo_s, glo_r, glo_y, glo_o, 64, lead, 2 * QS - 1)
        send_pair_y(QS - 1, 0)

    def f_block(f, _):
        gr2_s[f] = dot(block_rows(z1, f, 0, T // 128), cot[f]).astype(BF)
        return 0

    lax.fori_loop(0, 8, f_block, 0)
    every = pl.ds(0, 8)
    sum_x(gr2_s, gr2_r, 16, every, 2 * QS)

    def write_tile(z, tile_of, nat, j):
        for f in range(8):
            yt = dot_nt(eye, block_rows(z, f, j * 2, 2)).astype(BF)
            zo[pl.ds(f, TT, stride=8), :] = tile_of(yt, f)
        nat[quarter(j)] = zo[...].reshape(TT, 8, NB).astype(BF)

    def out_tile(j, _):
        write_tile(z1, lambda yt, f: dot(yt, r2g[f]), nat_o, j)
        return 0

    lax.fori_loop(0, T // TT, out_tile, 0)
    last_pair()
    sum_y(gr2_s, gr2_r, gr2_y, gr2_o, 16, every, 2 * QS)
    send_y(gr2_y, gr2_yr, every, 2 * QS)

    def back_tile(j):
        write_tile(z3, lambda yt, a: dot_nt(yt, lg[a]), nat_t, j)

    for a in range(8):
        gl_acc[a] = jnp.zeros((NB, NB), F32)

    def a_stage(j, _):
        await_bytes(s4.at[:, pl.ds(0, 240), quarter(j)], aa_r.at[3, j])
        gather_rows(s4, z3, j * 2, 2)
        for a in range(8):
            gl_acc[a] += dot(block_rows(z3, a, j * 2, 2), tok[a, quarter(j), :])
        return 0

    def a_early(j, _):
        a_stage(j, 0)
        back_tile(j)
        return 0

    lax.fori_loop(0, T // TT - 1, a_early, 0)
    a_stage(T // TT - 1, 0)
    for a in range(8):
        gl_s[:, a] = gl_acc[a].T.reshape(ND, 16, NB).astype(BF)

    def give(i, _):
        to, g = dpeer(i)
        remote(gl_s.at[to], gl_r.at[i - 1],
               rx_s.at[2 * QS + 1], rx_r.at[2 * QS + 1], (to, g)).start()
        return 0

    lax.fori_loop(1, ND, give, 0)
    back_tile(T // TT - 1)

    def fin(q, _):
        lead = pl.ds(q * 2, 2)
        finish(gr_yr, gr_o, lead, q)
        finish(glo_yr, glo_o, lead, QS + q)
        return 0

    lax.fori_loop(0, QS, fin, 0)
    finish(gr2_yr, gr2_o, every, 2 * QS)
    await_bytes(gl_r, rx_r.at[2 * QS + 1])
    total = gl_s[dp].astype(F32)
    for i in range(ND - 1):
        total += gl_r[i].astype(F32)
    gl_o[...] = total * scale

    for k, (sh, g, n) in enumerate(facs):
        await_bytes(g.at[:, pl.ds(0, n), :], agy_s.at[k])
        await_bytes(g.at[:, pl.ds(0, 6 * n), :], agx_s.at[k])

    def drain(q, _):
        for kind, buf in enumerate((a1, a3, a2)):
            await_bytes(buf.at[q, pl.ds(0, 240), :], aa_s.at[kind, q])
        await_bytes(a4.at[:, pl.ds(0, 240), quarter(q)], aa_s.at[3, q])
        lead = pl.ds(q * 2, 2)
        await_bytes(gr_r.at[:, lead], rx_s.at[q])
        await_bytes(glo_r.at[:, lead], rx_s.at[QS + q])
        await_bytes(gr_yr.at[lead], ry_s.at[q])
        await_bytes(glo_yr.at[lead], ry_s.at[QS + q])
        return 0

    lax.fori_loop(0, QS, drain, 0)
    await_bytes(gr2_r, rx_s.at[2 * QS])
    await_bytes(gl_r, rx_s.at[2 * QS + 1])
    await_bytes(gr2_yr, ry_s.at[2 * QS])


CUTS = (4, 4, 1, 1, 1, 1)


def copy_all(*refs):
    copies = []
    for i, cuts in enumerate(CUTS):
        n = refs[i].shape[0] // cuts
        for j in range(cuts):
            rows = pl.ds(j * n, n)
            copies.append(pltpu.make_async_copy(refs[i].at[rows], refs[6 + i].at[rows], refs[12].at[len(copies)]))
    for c in copies:
        c.start()
    for c in copies:
        c.wait()


def on_device(tokens, cotangent, left_up, right_up, left_out, right_out):
    any_, vm = pl.BlockSpec(memory_space=pl.ANY), pl.BlockSpec(memory_space=pltpu.VMEM)
    V, D = pltpu.VMEM, pltpu.SemaphoreType.DMA
    slab = V((QS, NF * 16, T), BF)
    scratch = [
        V((8, T, NB), BF), V((8, T, NB), BF),
        V((8, NB, NB), BF), V((8, NB, EX), BF), V((8, EX, NB), BF), V((8, NB, NB), BF),
        slab, slab, slab, slab, slab, slab, slab, slab,
        V((T // 128, 1024, 128), F32), V((T // 128, 1024, 128), F32),
        V((2, NB, T), BF), V((2, NB, T), BF), V((EX, NB), BF), V((NB, EX), BF),
        V((EX, T), BF), V((EX, T), BF), V((2, NB, T), F32), V((2, NB, T), F32),
        V((8, NB, EX), BF), V((8, EX, NB), BF), V((ND, 8, 16, NB), BF), V((8, NB, NB), BF),
        V((3, 8, 32, EX), BF), V((3, 8, 128, NB), BF), V((7, 8, 16, NB), BF), V((3, 8, 32, NB), BF),
        V((8, 16, EX), BF), V((8, 64, NB), BF), V((8, 16, NB), BF),
        V((8, 16, EX), BF), V((8, 64, NB), BF), V((8, 16, NB), BF),
        V((1024, 128), F32), V((TT * 8, NB), F32), V((8, NB, NB), F32),
        D((2,)), D((4,)),
        D((4,)), D((4,)), D((4,)), D((4,)), D((4, QS)), D((4, QS)),
        D((2 * QS + 2,)), D((2 * QS + 2,)), D((2 * QS + 1,)), D((2 * QS + 1,)),
    ]
    S = jax.ShapeDtypeStruct
    results = pl.pallas_call(
        layer,
        out_shape=(V((T, 8, NB), BF), V((T, 8, NB), BF), V((8, 16, NB), F32), V((8, 16, EX), F32),
                   V((8, 64, NB), F32), V((8, 16, NB), F32)),
        in_specs=[any_] * 6,
        out_specs=(vm,) * 6,
        scratch_shapes=scratch,
        compiler_params=pltpu.CompilerParams(collective_id=0, has_side_effects=True, vmem_limit_bytes=52 << 20),
        cost_estimate=pl.CostEstimate(flops=8 << 30, bytes_accessed=12 << 20, transcendentals=8 << 20),
        name="monarch_layer",
    )(tokens, cotangent, left_up, right_up, left_out, right_out)
    return pl.pallas_call(
        copy_all,
        out_shape=tuple(S(r.shape, r.dtype) for r in results),
        in_specs=[vm] * 6,
        out_specs=(any_,) * 6,
        scratch_shapes=[D((sum(CUTS),))],
        compiler_params=pltpu.CompilerParams(vmem_limit_bytes=1 << 20),
        name="copy_results",
    )(*[pltpu.with_memory_space_constraint(r, V) for r in results])


def solution(mesh):
    wide, narrow = P("dp", "feat", None), P("feat", "dp", None)
    return jax.shard_map(
        on_device,
        mesh=mesh,
        in_specs=(wide, wide, narrow, narrow, narrow, narrow),
        out_specs=(wide, wide, narrow, narrow, narrow, narrow),
        check_vma=False,
    )
```

```python
import functools

import jax
import jax.numpy as jnp
from jax import lax
from jax.experimental import pallas as pl
from jax.experimental.pallas import tpu as pltpu
from jax.sharding import PartitionSpec as P

MESH = pl.DeviceIdType.MESH
BF = jnp.bfloat16
F32 = jnp.float32
NB = 128
EX = 512
T = 1024
TT = 256
NF = 16
ND = 8
NX = 4
QS = 4
STEPS = ((1, 2, 0), (1, 2, 1), (1, 1, 0), (1, 3, 0), (1, 1, 1), (1, 3, 1), (1, 0, 0), (1, 0, 1),
         (0, 2, 0), (0, 2, 1), (0, 1, 0), (0, 3, 0), (0, 1, 1), (0, 3, 1), (0, 0, 1))
NT = (((1,), (1,)), ((), ()))


def dot(a, b):
    return jnp.dot(a, b, preferred_element_type=F32)


def dot_nt(a, b):
    return lax.dot_general(a, b, NT, preferred_element_type=F32)


def gelu_parts(v):
    bell = jnp.exp2(v * v * (-0.7213475204444817)) * 0.3989422804014327
    t = 1.0 / (1.0 + 0.2316419 * jnp.abs(v))
    poly = 1.330274429 * t - 1.821255978
    poly = poly * t + 1.781477937
    poly = poly * t - 0.356563782
    poly = poly * t + 0.319381530
    tail = bell * (poly * t)
    phi = jnp.where(v >= 0, 1.0 - tail, tail)
    return v * phi, phi + v * bell


def layer(tok_h, cot_h, l_h, r_h, lo_h, r2_h,
          nat_o, nat_t, gl_o, gr_o, glo_o, gr2_o,
          tok, cot, lg, rg, log_, r2g,
          a1, a3, a2, a4, s1, s3, s2, s4, z1, z3,
          xc, fc, rt, lot, act, bp, zf, zb,
          gr_s, glo_s, gl_s, gr2_s, gr_r, glo_r, gl_r, gr2_r,
          gr_y, glo_y, gr2_y, gr_yr, glo_yr, gr2_yr, zr, zo, gl_acc,
          in_sem, own_sem,
          agy_s, agy_r, agx_s, agx_r, aa_s, aa_r, rx_s, rx_r, ry_s, ry_r):
    dp = lax.axis_index("dp")
    me = lax.axis_index("feat")
    x, yh = lax.div(dp, 2), lax.rem(dp, 2)
    partner = (x * 2 + (1 - yh), me)

    def xpeer(i):
        return (lax.rem(x + i, NX) * 2 + yh, me)

    fy, fz, fc_ = lax.div(me, 8), lax.rem(lax.div(me, 2), 4), lax.rem(me, 2)

    def fpeer(step):
        dy, dz, dc = step
        return lax.rem(fy + dy, 2) * 8 + lax.rem(fz + dz, 4) * 2 + lax.rem(fc_ + dc, 2)

    ins = [pltpu.make_async_copy(tok_h, nat_o, in_sem.at[0]), pltpu.make_async_copy(cot_h, nat_t, in_sem.at[1])]
    for c in ins:
        c.start()
    facs = [(l_h, lg, 16), (r2_h, r2g, 16), (r_h, rg, 16), (lo_h, log_, 64)]
    own = [pltpu.make_async_copy(sh, g.at[:, pl.ds(pl.multiple_of(dp * n, n), n), :], own_sem.at[k])
           for k, (sh, g, n) in enumerate(facs)]
    for c in own:
        c.start()

    barrier = pltpu.get_barrier_semaphore()

    def dpeer(i):
        return (lax.rem(dp + i, ND), me)

    def greet(i, _):
        pl.semaphore_signal(barrier, inc=1, device_id=(dp, lax.rem(me + i, NF)), device_id_type=MESH)
        return 0

    lax.fori_loop(1, NF, greet, 0)

    def greet_group(i, _):
        pl.semaphore_signal(barrier, inc=1, device_id=dpeer(i), device_id_type=MESH)
        return 0

    lax.fori_loop(1, ND, greet_group, 0)
    pl.semaphore_wait(barrier, NF - 1 + ND - 1)

    def remote(src, dst, ss, rs, dev):
        return pltpu.make_async_remote_copy(src_ref=src, dst_ref=dst, send_sem=ss, recv_sem=rs,
                                            device_id=dev, device_id_type=MESH)

    def await_bytes(ref, sem):
        pltpu.make_async_copy(ref, ref, sem).wait()

    def share_y(k):
        sh, g, n = facs[k]
        mine = g.at[:, pl.ds(pl.multiple_of(dp * n, n), n), :]
        own[k].wait()
        remote(mine, mine, agy_s.at[k], agy_r.at[k], partner).start()

    def share_x(k):
        sh, g, n = facs[k]
        mine = g.at[:, pl.ds(pl.multiple_of(dp * n, n), n), :]
        for i in range(1, NX):
            remote(mine, mine, agx_s.at[k], agx_r.at[k], xpeer(i)).start()

    def forward_shard(k):
        sh, g, n = facs[k]
        theirs = g.at[:, pl.ds(pl.multiple_of(partner[0] * n, n), n), :]
        await_bytes(theirs, agy_r.at[k])
        for i in range(1, NX):
            remote(theirs, theirs, agx_s.at[k], agx_r.at[k], xpeer(i)).start()

    def gathered(k):
        sh, g, n = facs[k]
        await_bytes(g.at[:, pl.ds(0, 6 * n), :], agx_r.at[k])

    share_y(1)
    share_x(1)
    for k in (0, 2, 3):
        share_y(k)

    def relay(nat, dst):
        def one(j, _):
            rows = pl.ds(pl.multiple_of(j * 128, 128), 128)
            zr[...] = nat[rows].astype(F32).reshape(1024, 128)
            for a in range(8):
                dst[a, rows, :] = zr[pl.ds(a, 128, stride=8), :].astype(BF)
            return 0

        lax.fori_loop(0, T // 128, one, 0)

    forward_shard(1)
    share_x(0)
    ins[1].wait()
    relay(nat_t, cot)
    forward_shard(0)

    def spread(z, a, res, t0):
        for h in range(TT // 128):
            z[t0 // 128 + h, pl.ds(a, NB, stride=8), :] = res[:, h * 128:(h + 1) * 128]

    def send_pair(z, abuf, sbuf, kind, q, first=0, end=T // 128):
        def one(p, _):
            rows = pl.ds(pl.multiple_of(p * 16, 16), 16)
            for tt in range(first, end):
                piece = z[tt, pl.ds(pl.multiple_of(p * 64 + q * 16, 16), 16), :].astype(BF)
                abuf[q, rows, tt * 128:(tt + 1) * 128] = piece
            return 0

        lax.fori_loop(0, NF, one, 0)
        ship(abuf, sbuf, kind, q, pl.ds(first * 128, (end - first) * 128))

    def ship(abuf, sbuf, kind, q, cols=pl.ds(0, T)):
        mine = pl.ds(pl.multiple_of(me * 16, 16), 16)

        for step in STEPS:
            p = fpeer(step)
            rows = pl.ds(pl.multiple_of(p * 16, 16), 16)
            remote(abuf.at[q, rows, cols], sbuf.at[q, mine, cols], aa_s.at[kind, q], aa_r.at[kind, q], (dp, p)).start()
        sbuf[q, mine, cols] = abuf[q, mine, cols]

    def arrived(sbuf, kind, q):
        await_bytes(sbuf.at[q, pl.ds(0, 240), :], aa_r.at[kind, q])

    gathered(1)
    for first in (0, 4):
        for f in range(8):
            for t0 in range(first * 128, first * 128 + T // 2, TT):
                spread(z3, f, dot_nt(r2g[f], cot[f, t0:t0 + TT, :]), t0)
        send_pair(z3, a3, s3, 1, 0, first, first + 4)
    share_x(2)
    share_x(3)
    send_pair(z3, a3, s3, 1, 1)
    ins[0].wait()
    relay(nat_o, tok)
    gathered(0)
    for a in range(8):
        lt = lg[a].astype(F32).T.astype(BF)
        for t0 in range(0, T, TT):
            spread(z1, a, dot_nt(lt, tok[a, t0:t0 + TT, :]), t0)
    send_pair(z1, a1, s1, 0, 0)
    forward_shard(2)
    forward_shard(3)
    send_pair(z1, a1, s1, 0, 1)

    def rest(q, _):
        send_pair(z1, a1, s1, 0, q)
        send_pair(z3, a3, s3, 1, q)
        return 0

    lax.fori_loop(2, QS, rest, 0)
    gathered(2)
    gathered(3)

    def sum_x(src, dst, n, lead, sem):
        for i in range(1, NX):
            to = lax.rem(x + i, NX)
            remote(src.at[lead, pl.ds(pl.multiple_of(to * 2 * n, 2 * n), 2 * n), :], dst.at[i - 1, lead],
                   rx_s.at[sem], rx_r.at[sem], xpeer(i)).start()

    scale = 1.0 / jnp.sqrt(F32(8192.0))

    def sum_y(src, dst, ybuf, res, n, lead, sem):
        await_bytes(dst.at[:, lead], rx_r.at[sem])
        for half in range(2):
            total = src[lead, pl.ds(pl.multiple_of(x * 2 * n + half * n, n), n), :].astype(F32)
            for i in range(NX - 1):
                total += dst[i, lead, half * n:(half + 1) * n, :].astype(F32)

            @pl.when(yh == half)
            def _():
                res[lead] = total

            @pl.when(yh != half)
            def _():
                ybuf[lead] = total.astype(BF)

    def send_y(ybuf, yrecv, lead, sem):
        remote(ybuf.at[lead], yrecv.at[lead], ry_s.at[sem], ry_r.at[sem], partner).start()

    def finish(yrecv, res, lead, sem):
        await_bytes(yrecv.at[lead], ry_r.at[sem])
        res[lead] = (res[lead] + yrecv[lead].astype(F32)) * scale

    def pair(q, _):
        arrived(s1, 0, q)
        arrived(s3, 1, q)
        for t0 in range(0, T, TT):
            for src, dst in ((s1, xc), (s3, fc)):
                slab = src[q, :, t0:t0 + TT].astype(F32).reshape(NF, 2, 8, TT)
                for h in range(2):
                    dst[h, :, t0:t0 + TT] = slab[:, h].reshape(NB, TT).astype(BF)

        def block(h, _):
            c = q * 2 + h
            rt[...] = rg[c].astype(F32).T.astype(BF)
            lot[...] = log_[c].astype(F32).T.astype(BF)

            def tile(j, _):
                cols = pl.ds(pl.multiple_of(j * TT, TT), TT)
                active, slope = gelu_parts(dot(rt[...], xc[h, :, cols]))
                active = active.astype(BF)
                act[:, cols] = active
                back = (dot(log_[c], fc[h, :, cols]) * slope).astype(BF)
                bp[:, cols] = back
                zf[h, :, cols] = dot(lot[...], active)
                zb[h, :, cols] = dot(rg[c], back)
                return 0

            lax.fori_loop(0, T // TT, tile, 0)
            glo_s[c] = dot_nt(act[...], fc[h]).astype(BF)
            gr_s[c] = dot_nt(xc[h], bp[...]).astype(BF)
            return 0

        lax.fori_loop(0, 2, block, 0)

        for z, abuf, sbuf, kind in ((zf, a2, s2, 2), (zb, a4, s4, 3)):
            def pack(p, _):
                rows = pl.ds(pl.multiple_of(p * 8, 8), 8)
                both = jnp.concatenate([z[0, rows, :], z[1, rows, :]], axis=0)
                abuf[q, pl.ds(pl.multiple_of(p * 16, 16), 16), :] = both.astype(BF)
                return 0

            lax.fori_loop(0, NF, pack, 0)
            if kind == 2:
                ship(abuf, sbuf, kind, q)

        lead = pl.ds(q * 2, 2)
        sum_x(gr_s, gr_r, 16, lead, q)
        sum_x(glo_s, glo_r, 64, lead, QS + q)

        @pl.when(q > 0)
        def _():
            before = pl.ds(q * 2 - 2, 2)
            sum_y(gr_s, gr_r, gr_y, gr_o, 16, before, q - 1)
            sum_y(glo_s, glo_r, glo_y, glo_o, 64, before, QS + q - 1)

        return 0

    lax.fori_loop(0, QS, pair, 0)

    def quarter(j):
        return pl.ds(pl.multiple_of(j * TT, TT), TT)

    def ship_back(j, _):
        mine = pl.ds(pl.multiple_of(me * 16, 16), 16)

        for step in STEPS:
            p = fpeer(step)
            rows = pl.ds(pl.multiple_of(p * 16, 16), 16)
            remote(a4.at[:, rows, quarter(j)], s4.at[:, mine, quarter(j)], aa_s.at[3, j], aa_r.at[3, j], (dp, p)).start()
        s4[:, mine, quarter(j)] = a4[:, mine, quarter(j)]
        return 0

    lax.fori_loop(0, T // TT, ship_back, 0)

    def send_pair_y(q, _):
        lead = pl.ds(q * 2, 2)
        send_y(gr_y, gr_yr, lead, q)
        send_y(glo_y, glo_yr, lead, QS + q)
        return 0

    lax.fori_loop(0, QS - 1, send_pair_y, 0)

    def gather_rows(sbuf, z, first, count):
        def one_q(q, _):
            for k in range(NF):
                for i in range(count):
                    tt = first + i
                    slab = sbuf[q, k * 16:(k + 1) * 16, pl.ds(pl.multiple_of(tt * 128, 128), 128)].astype(F32)
                    for h in range(2):
                        z[tt, pl.ds(k * 8 + q * 2 + h, 8, stride=NB), :] = slab[h * 8:(h + 1) * 8]
            return 0

        lax.fori_loop(0, QS, one_q, 0)

    eye = (lax.broadcasted_iota(jnp.int32, (TT, TT), 0) == lax.broadcasted_iota(jnp.int32, (TT, TT), 1)).astype(BF)

    def block_rows(z, f, first, count):
        rows = pl.ds(pl.multiple_of(f * NB, NB), NB)
        return jnp.concatenate([z[first + i, rows, :].astype(BF) for i in range(count)], axis=1)

    def folded_here(q, _):
        arrived(s2, 2, q)
        return 0

    lax.fori_loop(0, QS, folded_here, 0)
    gather_rows(s2, z1, 0, T // 128)

    def last_pair():
        lead = pl.ds(QS * 2 - 2, 2)
        sum_y(gr_s, gr_r, gr_y, gr_o, 16, lead, QS - 1)
        sum_y(glo_s, glo_r, glo_y, glo_o, 64, lead, 2 * QS - 1)
        send_pair_y(QS - 1, 0)

    def f_block(f, _):
        gr2_s[f] = dot(block_rows(z1, f, 0, T // 128), cot[f]).astype(BF)
        return 0

    lax.fori_loop(0, 8, f_block, 0)
    every = pl.ds(0, 8)
    sum_x(gr2_s, gr2_r, 16, every, 2 * QS)

    def write_tile(z, tile_of, nat, j):
        for f in range(8):
            yt = dot_nt(eye, block_rows(z, f, j * 2, 2)).astype(BF)
            zo[pl.ds(f, TT, stride=8), :] = tile_of(yt, f)
        nat[quarter(j)] = zo[...].reshape(TT, 8, NB).astype(BF)

    def out_tile(j, _):
        write_tile(z1, lambda yt, f: dot(yt, r2g[f]), nat_o, j)
        return 0

    lax.fori_loop(0, T // TT, out_tile, 0)
    last_pair()
    sum_y(gr2_s, gr2_r, gr2_y, gr2_o, 16, every, 2 * QS)
    send_y(gr2_y, gr2_yr, every, 2 * QS)

    def back_tile(j):
        write_tile(z3, lambda yt, a: dot_nt(yt, lg[a]), nat_t, j)

    for a in range(8):
        gl_acc[a] = jnp.zeros((NB, NB), F32)

    def a_stage(j, _):
        await_bytes(s4.at[:, pl.ds(0, 240), quarter(j)], aa_r.at[3, j])
        gather_rows(s4, z3, j * 2, 2)
        for a in range(8):
            gl_acc[a] += dot(block_rows(z3, a, j * 2, 2), tok[a, quarter(j), :])
        return 0

    def a_early(j, _):
        a_stage(j, 0)
        back_tile(j)
        return 0

    lax.fori_loop(0, T // TT - 1, a_early, 0)
    last = T // TT - 1
    await_bytes(s4.at[:, pl.ds(0, 240), quarter(last)], aa_r.at[3, last])
    gather_rows(s4, z3, last * 2, 2)
    for half in range(2):
        for a in range(half * 4, half * 4 + 4):
            term = gl_acc[a] + dot(block_rows(z3, a, last * 2, 2), tok[a, quarter(last), :])
            gl_s[:, a] = term.T.reshape(ND, 16, NB).astype(BF)

        def give(i, _):
            to, g = dpeer(i)
            part = pl.ds(half * 4, 4)
            remote(gl_s.at[to, part], gl_r.at[i - 1, part],
                   rx_s.at[2 * QS + 1], rx_r.at[2 * QS + 1], (to, g)).start()
            return 0

        lax.fori_loop(1, ND, give, 0)

    back_tile(T // TT - 1)

    def fin(q, _):
        lead = pl.ds(q * 2, 2)
        finish(gr_yr, gr_o, lead, q)
        finish(glo_yr, glo_o, lead, QS + q)
        return 0

    lax.fori_loop(0, QS, fin, 0)
    finish(gr2_yr, gr2_o, every, 2 * QS)
    await_bytes(gl_r, rx_r.at[2 * QS + 1])
    total = gl_s[dp].astype(F32)
    for i in range(ND - 1):
        total += gl_r[i].astype(F32)
    gl_o[...] = total * scale

    for k, (sh, g, n) in enumerate(facs):
        await_bytes(g.at[:, pl.ds(0, n), :], agy_s.at[k])
        await_bytes(g.at[:, pl.ds(0, 6 * n), :], agx_s.at[k])

    def drain(q, _):
        for kind, buf in enumerate((a1, a3, a2)):
            await_bytes(buf.at[q, pl.ds(0, 240), :], aa_s.at[kind, q])
        await_bytes(a4.at[:, pl.ds(0, 240), quarter(q)], aa_s.at[3, q])
        lead = pl.ds(q * 2, 2)
        await_bytes(gr_r.at[:, lead], rx_s.at[q])
        await_bytes(glo_r.at[:, lead], rx_s.at[QS + q])
        await_bytes(gr_yr.at[lead], ry_s.at[q])
        await_bytes(glo_yr.at[lead], ry_s.at[QS + q])
        return 0

    lax.fori_loop(0, QS, drain, 0)
    await_bytes(gr2_r, rx_s.at[2 * QS])
    await_bytes(gl_r, rx_s.at[2 * QS + 1])
    await_bytes(gr2_yr, ry_s.at[2 * QS])


CUTS = (4, 4, 1, 1, 1, 1)


def copy_all(*refs):
    copies = []
    for i, cuts in enumerate(CUTS):
        n = refs[i].shape[0] // cuts
        for j in range(cuts):
            rows = pl.ds(j * n, n)
            copies.append(pltpu.make_async_copy(refs[i].at[rows], refs[6 + i].at[rows], refs[12].at[len(copies)]))
    for c in copies:
        c.start()
    for c in copies:
        c.wait()


def on_device(tokens, cotangent, left_up, right_up, left_out, right_out):
    any_, vm = pl.BlockSpec(memory_space=pl.ANY), pl.BlockSpec(memory_space=pltpu.VMEM)
    V, D = pltpu.VMEM, pltpu.SemaphoreType.DMA
    slab = V((QS, NF * 16, T), BF)
    scratch = [
        V((8, T, NB), BF), V((8, T, NB), BF),
        V((8, NB, NB), BF), V((8, NB, EX), BF), V((8, EX, NB), BF), V((8, NB, NB), BF),
        slab, slab, slab, slab, slab, slab, slab, slab,
        V((T // 128, 1024, 128), F32), V((T // 128, 1024, 128), F32),
        V((2, NB, T), BF), V((2, NB, T), BF), V((EX, NB), BF), V((NB, EX), BF),
        V((EX, T), BF), V((EX, T), BF), V((2, NB, T), F32), V((2, NB, T), F32),
        V((8, NB, EX), BF), V((8, EX, NB), BF), V((ND, 8, 16, NB), BF), V((8, NB, NB), BF),
        V((3, 8, 32, EX), BF), V((3, 8, 128, NB), BF), V((7, 8, 16, NB), BF), V((3, 8, 32, NB), BF),
        V((8, 16, EX), BF), V((8, 64, NB), BF), V((8, 16, NB), BF),
        V((8, 16, EX), BF), V((8, 64, NB), BF), V((8, 16, NB), BF),
        V((1024, 128), F32), V((TT * 8, NB), F32), V((8, NB, NB), F32),
        D((2,)), D((4,)),
        D((4,)), D((4,)), D((4,)), D((4,)), D((4, QS)), D((4, QS)),
        D((2 * QS + 2,)), D((2 * QS + 2,)), D((2 * QS + 1,)), D((2 * QS + 1,)),
    ]
    S = jax.ShapeDtypeStruct
    results = pl.pallas_call(
        layer,
        out_shape=(V((T, 8, NB), BF), V((T, 8, NB), BF), V((8, 16, NB), F32), V((8, 16, EX), F32),
                   V((8, 64, NB), F32), V((8, 16, NB), F32)),
        in_specs=[any_] * 6,
        out_specs=(vm,) * 6,
        scratch_shapes=scratch,
        compiler_params=pltpu.CompilerParams(collective_id=0, has_side_effects=True, vmem_limit_bytes=52 << 20),
        cost_estimate=pl.CostEstimate(flops=8 << 30, bytes_accessed=12 << 20, transcendentals=8 << 20),
        name="monarch_layer",
    )(tokens, cotangent, left_up, right_up, left_out, right_out)
    return pl.pallas_call(
        copy_all,
        out_shape=tuple(S(r.shape, r.dtype) for r in results),
        in_specs=[vm] * 6,
        out_specs=(any_,) * 6,
        scratch_shapes=[D((sum(CUTS),))],
        compiler_params=pltpu.CompilerParams(vmem_limit_bytes=1 << 20),
        name="copy_results",
    )(*[pltpu.with_memory_space_constraint(r, V) for r in results])


def solution(mesh):
    wide, narrow = P("dp", "feat", None), P("feat", "dp", None)
    return jax.shard_map(
        on_device,
        mesh=mesh,
        in_specs=(wide, wide, narrow, narrow, narrow, narrow),
        out_specs=(wide, wide, narrow, narrow, narrow, narrow),
        check_vma=False,
    )
```
